32 devices in a mesh: batch: 8 (over z, y), seq: 4 (over x, core).
Axes of the slice: x: 2, y: 2, z: 4, core: 2. Of those that a mesh axis runs over, the one named last changes fastest.
Arguments:
- tokens: bfloat16 [24, 512, 768], P('batch', 'seq'), may hold values from -6 to 6
- cotangent: bfloat16 [24, 512, 768], P('batch', 'seq'), may hold values from -6 to 6
- path_masks: int32 [24, 5], P('batch'), may hold values from 0 to 1, as said below
- seg_starts: int32 [24, 4], P('batch'), may hold values from 0 to 511, as said below
- query_weight: bfloat16 [768, 768], replicated, may hold values from -0.21875 to 0.21875
- key_weight: bfloat16 [768, 768], replicated, may hold values from -0.21875 to 0.21875
- value_weight: bfloat16 [768, 768], replicated, may hold values from -0.21875 to 0.21875
- output_weight: bfloat16 [768, 768], replicated, may hold values from -1.75 to 1.75
- small_kernel: bfloat16 [3, 768], replicated, may hold values from -3.5 to 3.5
- middle_kernel: bfloat16 [5, 768], replicated, may hold values from -2.5 to 2.5
- large_kernel: bfloat16 [7, 768], replicated, may hold values from -2 to 2
- small_mixer: bfloat16 [768, 768], replicated, may hold values from -0.21875 to 0.21875
- middle_mixer: bfloat16 [768, 768], replicated, may hold values from -0.21875 to 0.21875
- large_mixer: bfloat16 [768, 768], replicated, may hold values from -0.21875 to 0.21875
- inner_weight: bfloat16 [768, 3072], replicated, may hold values from -0.21875 to 0.21875
- outer_weight: bfloat16 [3072, 768], replicated, may hold values from -0.109375 to 0.109375
- norm_gain: bfloat16 [768], replicated, may hold values from 0.5 to 1.5
- norm_bias: bfloat16 [768], replicated, may hold values from -1.5 to 1.5
Outputs:
- block_output: bfloat16 [24, 512, 768], P('batch', 'seq')
- input_grad: bfloat16 [24, 512, 768], P('batch', 'seq')
- query_grad: float32 [768, 768], P('batch')
- key_grad: float32 [768, 768], P('batch')
- value_grad: float32 [768, 768], P('batch')
- output_grad: float32 [768, 768], P('batch')
- small_kernel_grad: float32 [3, 768], P(None, 'batch')
- middle_kernel_grad: float32 [5, 768], P(None, 'batch')
- large_kernel_grad: float32 [7, 768], P(None, 'batch')
- small_mixer_grad: float32 [768, 768], P('batch')
- middle_mixer_grad: float32 [768, 768], P('batch')
- large_mixer_grad: float32 [768, 768], P('batch')
- inner_grad: float32 [768, 3072], P('batch')
- outer_grad: float32 [3072, 768], P('batch')
- gain_grad: float32 [768], P('batch')
- bias_grad: float32 [768], P('batch')
The draws below stay inside these ranges and needn't reach their ends.
Inputs may be any that keep to these rules, and one draw needn't show every extreme that they name: `path_masks`: every entry is 0 or 1, and every column has a 1 in some row. `seg_starts`: each row begins with 0 and never falls; equal starts mean empty documents.
All inputs are finite; a program needn't handle non-finite values.
Results may differ from the reference program's by a relative error of at most 0.012.
The reference program's roundings to bfloat16 on the way count: a program that leaves them out, or rounds other values in their place, can miss the bound.
Values may be sent and summed in bfloat16 or wider, within the bound.
No kernel may reach another device: no remote copies, remote signals or barrier semaphores. Data moves between devices by JAX's collectives and lax.ppermute only.
A program may use at most 192 MiB of HBM per device.

```python
import math
import jax
import jax.numpy as jnp
from jax import lax

D = 768
H = 12
HD = 64
FF = 3072
LEN = 512
DOCS = 4
OPS = 5
SEQS = 3
SEQS_ALL = 24


def draw_path_masks(key, part):
    total_rows = SEQS_ALL
    row_index = jnp.arange(total_rows, dtype=jnp.int32)[:, None]
    column = jnp.arange(OPS, dtype=jnp.int32)[None, :]
    level = jnp.where(column % 2 == 0, row_index, total_rows - 1 - row_index)
    drawn = jax.random.randint(key, (total_rows, OPS), 0, 4 * total_rows)
    chosen = (drawn < total_rows + 2 * level).astype(jnp.int32)
    forced = (row_index == column).astype(jnp.int32)
    return jnp.maximum(chosen, forced)


def draw_seg_starts(key, part):
    total_rows = SEQS_ALL
    first, second, third, fourth = jax.random.split(key, 4)
    others = jnp.sort(jax.random.randint(first, (total_rows, DOCS - 1), 1, LEN), axis=1)
    row_index = jnp.arange(total_rows, dtype=jnp.int32)
    picked = jax.random.randint(second, (total_rows // SEQS,), 0, SEQS)
    chosen = row_index % SEQS == picked[row_index // SEQS]
    early = jax.random.randint(third, (total_rows, 1), 1, LEN // 4)
    late = jnp.sort(jax.random.randint(fourth, (total_rows, DOCS - 3), 3 * LEN // 4 + 1, LEN - 1), axis=1)
    closing = jnp.full((total_rows, 1), LEN - 1, jnp.int32)
    forced = jnp.concatenate([early, late, closing], axis=1)
    others = jnp.where(chosen[:, None], forced, others)
    return jnp.concatenate([jnp.zeros((total_rows, 1), jnp.int32), others], axis=1)


def spiked(values, rng, source, target, blocks, factor):
    owner, partner = [(jnp.arange(values.shape[dim]) // (values.shape[dim] // blocks)).reshape([-1 if axis == dim else 1 for axis in range(values.ndim)]) for dim in (source, target)]
    chosen = jax.random.permutation(rng, blocks)[partner]
    strong = (owner == chosen) | (owner == (partner + blocks // 2) % blocks)
    return jnp.where(strong, factor * values, values)


def steps_of(stream_key, dims, cuts, least, top_value):
    loudness = 1.0
    for dim, shards_of in cuts:
        steps = jax.random.uniform(jax.random.fold_in(jax.random.fold_in(stream_key, 6), dim), (shards_of,), jnp.float32, least / len(cuts), top_value / len(cuts))
        loudness = loudness * jnp.repeat(jnp.exp(steps), dims[dim] // shards_of).reshape((-1,) + (1,) * (len(dims) - 1 - dim))
    return loudness


def normal_values(rng, extent, scale, bound, shards=(), kind=jnp.bfloat16):
    array = jax.random.normal(rng, extent, jnp.float32) * scale
    if len(shards) > 0:
        array = steps_of(rng, extent, shards, -0.22, 0.18) * array
    return jnp.clip(array, min=-bound, max=bound).astype(kind)


def gaussian_with(key, extent, deviation, most, cuts, heavy, kind=jnp.bfloat16):
    values = deviation * jax.random.normal(key, extent, jnp.float32)
    if cuts:
        values = values * steps_of(key, extent, cuts, -0.22, 0.18)
    return jnp.clip(spiked(values, jax.random.fold_in(key, 3), *heavy), -most, most).astype(kind)


def setup_inputs(seed: int = 0) -> dict:
    arg_keys = jax.random.split(jax.random.key(seed), 19)
    return {
        "tokens": gaussian_with(arg_keys[0], (SEQS_ALL, LEN, D), 1.0, 6.0, ((0, 8), (1, 4)), (0, 2, 8, 2.0)),
        "cotangent": gaussian_with(arg_keys[1], (SEQS_ALL, LEN, D), 1.0, 6.0, ((0, 8), (1, 4)), (0, 2, 8, 2.0)),
        "path_masks": draw_path_masks(jax.random.fold_in(arg_keys[18], 71), 0),
        "seg_starts": draw_seg_starts(jax.random.fold_in(arg_keys[18], 71), 0),
        "query_weight": normal_values(arg_keys[4], (D, D), D ** -0.5, 0.21875),
        "key_weight": normal_values(arg_keys[5], (D, D), D ** -0.5, 0.21875),
        "value_weight": normal_values(arg_keys[6], (D, D), D ** -0.5, 0.21875),
        "output_weight": normal_values(arg_keys[7], (D, D), H ** -0.5, 1.75),
        "small_kernel": normal_values(arg_keys[8], (3, D), 3 ** -0.5, 3.5),
        "middle_kernel": normal_values(arg_keys[9], (5, D), 5 ** -0.5, 2.5),
        "large_kernel": normal_values(arg_keys[10], (7, D), 7 ** -0.5, 2.0),
        "small_mixer": normal_values(arg_keys[11], (D, D), D ** -0.5, 0.21875),
        "middle_mixer": normal_values(arg_keys[12], (D, D), D ** -0.5, 0.21875),
        "large_mixer": normal_values(arg_keys[13], (D, D), D ** -0.5, 0.21875),
        "inner_weight": normal_values(arg_keys[14], (D, FF), D ** -0.5, 0.21875),
        "outer_weight": normal_values(arg_keys[15], (FF, D), FF ** -0.5, 0.109375),
        "norm_gain": jnp.clip(1.0 + 0.1 * jax.random.normal(arg_keys[16], (D,), jnp.float32), 0.5, 1.5).astype(jnp.bfloat16),
        "norm_bias": normal_values(arg_keys[17], (D,), 0.3, 1.5),
    }


HIGHEST = lax.Precision.HIGHEST
EPSILON = 1e-05
MASKED = -1e+30

@jax.custom_vjp
def low(v):
    return lax.optimization_barrier(v.astype(jnp.bfloat16)).astype(jnp.float32)

@jax.custom_vjp
def low_back(v):
    return v

def low_keep(v):
    return (low(v), None)

def low_pass(kept, grad):
    return (grad,)

def back_keep(v):
    return (v, None)

def back_low(kept, grad):
    return (low(grad),)
low.defvjp(low_keep, low_pass)
low_back.defvjp(back_keep, back_low)

def document_ids(starts, seq_len):
    positions = jnp.arange(seq_len, dtype=jnp.int32)
    inside = (starts[:, None, :] <= positions[None, :, None]).astype(jnp.int32)
    return lax.optimization_barrier(jnp.sum(inside, axis=2)) - 1

def project(matrix, weight):
    return jnp.dot(matrix, weight, precision=HIGHEST)

def attend_one(pieces):
    query_seq, keys_seq, values_seq, seq_docs = pieces
    seq_len = query_seq.shape[0]
    query_heads = query_seq.reshape(seq_len, H, HD)
    key_heads = keys_seq.reshape(seq_len, H, HD)
    value_heads = values_seq.reshape(seq_len, H, HD)
    scores = jnp.einsum('qhd,khd->hqk', query_heads, key_heads, precision=HIGHEST) * HD ** (-0.5)
    scores = low_back(scores)
    linked = seq_docs[:, None] == seq_docs[None, :]
    scores = jnp.where(linked[None], scores, MASKED)
    attn_probs = jax.nn.softmax(scores, axis=-1)
    attended = jnp.einsum('hqk,khd->qhd', low(attn_probs), value_heads, precision=HIGHEST)
    return attended.reshape(seq_len, H * HD)

def depthwise(inputs, kernel, seq_docs):
    tap_count = kernel.shape[0]
    half_taps = tap_count // 2
    seq_len = inputs.shape[1]
    padded = jnp.pad(inputs, ((0, 0), (half_taps, half_taps), (0, 0)))
    padded_docs = jnp.pad(seq_docs, ((0, 0), (half_taps, half_taps)), constant_values=-1)
    result = jnp.zeros(inputs.shape, jnp.float32)
    for offset in range(tap_count):
        linked = padded_docs[:, offset:offset + seq_len] == seq_docs
        result = result + jnp.where(linked[:, :, None], padded[:, offset:offset + seq_len], 0.0) * kernel[offset]
    return result

def block(inputs, params, masks_group, docs_group):
    query_weight, key_weight, value_weight, output_weight, small_kernel, middle_kernel, large_kernel, small_mixer, middle_mixer, large_mixer, inner_weight, outer_weight, norm_gain, norm_bias = params
    group_size, seq_len, model_dim = inputs.shape
    token_rows = inputs.reshape(group_size * seq_len, model_dim)

    def heads_in(weight):
        return low(low_back(project(token_rows, weight))).reshape(group_size, seq_len, model_dim)
    query_rows = heads_in(query_weight)
    key_rows = heads_in(key_weight)
    value_rows = heads_in(value_weight)
    attended = lax.map(jax.checkpoint(attend_one), (query_rows, key_rows, value_rows, docs_group))
    attended = low(low_back(attended)).reshape(group_size * seq_len, model_dim)
    branches = [low_back(project(attended, output_weight))]
    for kernel, mixer_weight in ((small_kernel, small_mixer), (middle_kernel, middle_mixer), (large_kernel, large_mixer)):
        conv_rows = low(low_back(depthwise(inputs, kernel, docs_group)))
        branches.append(low_back(project(conv_rows.reshape(group_size * seq_len, model_dim), mixer_weight)))
    hidden = low_back(project(token_rows, inner_weight))
    activated = low(low_back(jax.nn.gelu(hidden, approximate=False)))
    branches.append(low_back(project(activated, outer_weight)))
    summed = inputs
    for position in range(len(branches)):
        summed = summed + masks_group[:, position][:, None, None] * branches[position].reshape(group_size, seq_len, model_dim)
    centre = lax.optimization_barrier(jnp.mean(summed, axis=-1, keepdims=True))
    centred = summed - centre
    spread = lax.optimization_barrier(jnp.mean(centred * centred, axis=-1, keepdims=True))
    normed = centred * lax.rsqrt(spread + EPSILON)
    return normed * norm_gain + norm_bias

def reference(tokens, cotangent, path_masks, seg_starts, query_weight, key_weight, value_weight, output_weight, small_kernel, middle_kernel, large_kernel, small_mixer, middle_mixer, large_mixer, inner_weight, outer_weight, norm_gain, norm_bias):
    all_seqs, seq_len, model_dim = tokens.shape
    group_size = math.gcd(all_seqs, 8)
    group_count = all_seqs // group_size
    weights = tuple((weight_item.astype(jnp.float32) for weight_item in (query_weight, key_weight, value_weight, output_weight, small_kernel, middle_kernel, large_kernel, small_mixer, middle_mixer, large_mixer, inner_weight, outer_weight, norm_gain, norm_bias)))
    seq_docs = document_ids(seg_starts, seq_len)
    mask_values = path_masks.astype(jnp.float32)

    def grouped(values):
        return values.reshape((group_count, group_size) + values.shape[1:])

    def step_group(carried, pieces):
        inputs, upstream, masks_group, docs_group = pieces

        def forward(inputs_full, *params):
            return block(inputs_full, params, masks_group, docs_group)
        outputs, pullback = jax.vjp(forward, inputs.astype(jnp.float32), *weights)
        gradients = pullback(upstream.astype(jnp.float32))
        carried = tuple((before + after for before, after in zip(carried, gradients[1:])))
        return (carried, (outputs.astype(jnp.bfloat16), gradients[0].astype(jnp.bfloat16)))
    initial = tuple((jnp.zeros(weight_item.shape, jnp.float32) for weight_item in weights))
    totals, (outputs, input_grad) = lax.scan(step_group, initial, (grouped(tokens), grouped(cotangent), grouped(mask_values), grouped(seq_docs)))
    counts = lax.optimization_barrier(jnp.sum(mask_values, axis=0))
    owners = (0, 0, 0, 0, 1, 2, 3, 1, 2, 3, 4, 4)
    scaled = [totals[position] / counts[owners[position]] for position in range(12)]
    return (outputs.reshape(tokens.shape), input_grad.reshape(tokens.shape), scaled[0], scaled[1], scaled[2], scaled[3], scaled[4], scaled[5], scaled[6], scaled[7], scaled[8], scaled[9], scaled[10], scaled[11], totals[12], totals[13])
```

```python
import functools

import jax
import jax.numpy as jnp
from jax import lax
from jax.experimental import pallas as pl
from jax.experimental.pallas import tpu as pltpu
from jax.sharding import PartitionSpec as P

HD = 64
EPSILON = 1e-05
MASKED = -1e30
TAPS = (3, 5, 7)
F32 = jnp.float32
BF16 = jnp.bfloat16
VMEM_LIMIT = 56 * 1024 * 1024


def dot_nn(left, right):
    return jnp.dot(left, right, preferred_element_type=F32)


def dot_nt(left, right):
    return lax.dot_general(left, right, (((1,), (1,)), ((), ())), preferred_element_type=F32)


def dot_tn(left, right):
    return lax.dot_general(left, right, (((0,), (0,)), ((), ())), preferred_element_type=F32)


def doc_of(starts_ref, row, positions):
    found = jnp.zeros(positions.shape, jnp.int32)
    for which in range(starts_ref.shape[1]):
        found = found + (starts_ref[row, which] <= positions).astype(jnp.int32)
    return found


def assemble(full_ref, pieces, g, rows):
    for k, piece in enumerate(pieces):
        full_ref[0, pl.ds(pl.multiple_of((g ^ k) * rows, rows), rows), :] = piece[0]


def channels(out_ref, source, g, count, width, pad):
    length = source.shape[0]
    out_ref[0:pad, :] = jnp.zeros((pad, width), F32)
    out_ref[pad + length : 2 * pad + length, :] = jnp.zeros((pad, width), F32)
    for which in range(count):

        @pl.when(g == which)
        def _():
            out_ref[pad : pad + length, :] = source[:, which * width : (which + 1) * width].astype(F32)


def forward_kernel(
    count, g_ref, masks_ref, starts_ref, t0, t1, t2, t3, wqkv_ref, win_ref, wrow_ref, taps_ref,
    p0, p1, p2, p3, tok_ref, mcat_ref, slope_ref, qkv_ref, probs_ref, scaled_ref, chan_ref, part_ref,
):
    step = pl.program_id(0)
    g = g_ref[0]
    rows = t0.shape[1]
    length = tok_ref.shape[1]
    ffn = win_ref.shape[1]
    width = wqkv_ref.shape[1] // 3
    heads = width // HD
    assemble(tok_ref, (t0, t1, t2, t3), g, rows)
    masks = [masks_ref[step, c].astype(F32) for c in range(5)]

    qkv = dot_nn(tok_ref[0], wqkv_ref[...]).astype(BF16)
    qkv_ref[0, :, 0:width] = qkv[:, 0:width] * jnp.asarray(HD**-0.5, BF16)
    qkv_ref[0, :, width:] = qkv[:, width:]

    key_docs = doc_of(starts_ref, step, lax.broadcasted_iota(jnp.int32, (1, length), 1))
    tile = length // 4
    ones = jnp.ones((length, HD), BF16)
    for h in range(heads):
        keys = qkv_ref[0, :, width + h * HD : width + (h + 1) * HD]
        values = jnp.concatenate([qkv_ref[0, :, 2 * width + h * HD : 2 * width + (h + 1) * HD], ones], axis=1)

        def attend(i, carry, h=h, keys=keys, values=values):
            start = pl.multiple_of(i * tile, tile)
            docs = doc_of(starts_ref, step, start + lax.broadcasted_iota(jnp.int32, (tile, 1), 0))
            scores = dot_nt(qkv_ref[0, pl.ds(start, tile), h * HD : (h + 1) * HD], keys)
            scores = jnp.where(docs == key_docs, scores, MASKED)
            top = jnp.max(scores, axis=1, keepdims=True)
            weights = jnp.exp(scores - top)
            total = jnp.sum(weights, axis=1, keepdims=True)
            low = (weights * (1.0 / total)).astype(BF16)
            probs_ref[0, h, pl.ds(start, tile), :] = low
            both = dot_nn(low, values)
            attended = both[:, 0:HD]
            scaled_ref[0, pl.ds(start, tile), h * HD : (h + 1) * HD] = attended / both[:, HD : 2 * HD]
            mcat_ref[0, pl.ds(start, tile), ffn + h * HD : ffn + (h + 1) * HD] = (
                attended.astype(BF16) * masks[0].astype(BF16)
            )
            return carry

        lax.fori_loop(0, length // tile, attend, 0)

    pad = 8
    channels(chan_ref, tok_ref.at[0], g, count, width, pad)
    for start in range(0, length, 128):
        sums = [jnp.zeros((128, width), F32) for _ in TAPS]
        here = start + lax.broadcasted_iota(jnp.int32, (128, 1), 0)
        docs = doc_of(starts_ref, step, here)
        for shift in range(-3, 4):
            moved = chan_ref[pad + start + shift : pad + start + shift + 128, :]
            if shift != 0:
                moved = jnp.where(docs == doc_of(starts_ref, step, here + shift), moved, 0.0)
            base = 0
            for k, taps in enumerate(TAPS):
                if abs(shift) <= taps // 2:
                    tap = base + shift + taps // 2
                    sums[k] = sums[k] + moved * taps_ref[tap : tap + 1, :]
                base += taps
        for k in range(3):
            lane = ffn + (k + 1) * width
            mcat_ref[0, start : start + 128, lane : lane + width] = (sums[k] * masks[k + 1]).astype(BF16)

    def feed(i, carry):
        start = pl.multiple_of(i * 128, 128)
        hidden = dot_nn(tok_ref[0, pl.ds(start, 128), :], win_ref[...])
        cdf = 0.5 * (1.0 + lax.erf(hidden * (0.5**0.5)))
        density = jnp.exp(-0.5 * hidden * hidden) * 0.3989422804014327
        mcat_ref[0, pl.ds(start, 128), 0:ffn] = (hidden * cdf * masks[4]).astype(BF16)
        slope_ref[0, pl.ds(start, 128), :] = cdf + hidden * density
        return carry

    lax.fori_loop(0, length // 128, feed, 0)

    part_ref[...] = dot_nn(mcat_ref[0], wrow_ref[...])
    for k, out in enumerate((p0, p1, p2, p3)):
        out[0] = part_ref[pl.ds(pl.multiple_of((g ^ k) * rows, rows), rows), :].astype(BF16)


def norm_kernel(tok_ref, a_ref, b_ref, c_ref, cot_ref, gain_ref, bias_ref, out_ref, grad_ref, low_ref, sums_ref):
    step = pl.program_id(0)
    summed = tok_ref[0].astype(F32) + (a_ref[0].astype(F32) + b_ref[0].astype(F32) + c_ref[0].astype(F32))
    centred = summed - jnp.mean(summed, axis=1, keepdims=True)
    inverse = lax.rsqrt(jnp.mean(centred * centred, axis=1, keepdims=True) + EPSILON)
    normed = centred * inverse
    gain = gain_ref[...].astype(F32)
    out_ref[0] = (normed * gain + bias_ref[...].astype(F32)).astype(BF16)
    upstream = cot_ref[0].astype(F32)

    @pl.when(step == 0)
    def _():
        sums_ref[...] = jnp.zeros(sums_ref.shape, F32)

    sums_ref[0:1, :] += jnp.sum(upstream * normed, axis=0, keepdims=True)
    sums_ref[1:2, :] += jnp.sum(upstream, axis=0, keepdims=True)
    scaled = upstream * gain
    grad = inverse * (
        scaled
        - jnp.mean(scaled, axis=1, keepdims=True)
        - normed * jnp.mean(scaled * normed, axis=1, keepdims=True)
    )
    grad_ref[0] = grad
    low_ref[0] = grad.astype(BF16)


def backward_kernel(
    count, g_ref, masks_ref, starts_ref, l0, l1, l2, l3, tok_ref, slope_ref, qkv_ref, probs_ref, scaled_ref,
    wrow_ref, wcat_ref, taps_ref,
    p0, p1, p2, p3, acts_ref, tapsum_ref, low_ref, up_ref, chan_ref, c3_ref, c5_ref, c7_ref, part_ref,
):
    step = pl.program_id(0)
    g = g_ref[0]
    rows = l0.shape[1]
    length = tok_ref.shape[1]
    ffn = slope_ref.shape[2]
    width = qkv_ref.shape[2] // 3
    heads = width // HD
    pad = 8
    assemble(low_ref, (l0, l1, l2, l3), g, rows)
    masks = [masks_ref[step, c].astype(F32) for c in range(5)]

    def feed(i, carry):
        start = pl.multiple_of(i * 128, 128)
        grads = dot_nt(low_ref[0, pl.ds(start, 128), :], wrow_ref[0:ffn, :])
        grads = (grads * masks[4]).astype(BF16).astype(F32)
        acts_ref[0, pl.ds(start, 128), 0:ffn] = (grads * slope_ref[0, pl.ds(start, 128), :]).astype(BF16)
        return carry

    lax.fori_loop(0, length // 128, feed, 0)

    ups = dot_nt(low_ref[0], wrow_ref[ffn:, :])
    up_ref[...] = (ups[:, 0:width] * masks[0]).astype(BF16)
    conv_refs = (c3_ref, c5_ref, c7_ref)
    for k, ref in enumerate(conv_refs):
        ref[0:pad, :] = jnp.zeros((pad, width), F32)
        ref[pad + length : 2 * pad + length, :] = jnp.zeros((pad, width), F32)
        ref[pad : pad + length, :] = (
            (ups[:, (k + 1) * width : (k + 2) * width] * masks[k + 1]).astype(BF16).astype(F32)
        )

    tile = length // 2
    for h in range(heads):
        keys = qkv_ref[0, :, width + h * HD : width + (h + 1) * HD]
        values = qkv_ref[0, :, 2 * width + h * HD : 2 * width + (h + 1) * HD]
        key_sum = jnp.zeros((HD, length), F32)
        value_sum = jnp.zeros((HD, length), F32)
        for start in range(0, length, tile):
            query = qkv_ref[0, start : start + tile, h * HD : (h + 1) * HD]
            up = up_ref[start : start + tile, h * HD : (h + 1) * HD]
            low = probs_ref[0, h, start : start + tile, :]
            shared = jnp.sum(
                up.astype(F32) * scaled_ref[0, start : start + tile, h * HD : (h + 1) * HD], axis=1, keepdims=True
            )
            grads = (low.astype(F32) * (dot_nt(up, values) - shared)).astype(BF16)
            acts_ref[0, start : start + tile, ffn + h * HD : ffn + (h + 1) * HD] = (
                dot_nn(grads, keys) * (HD**-0.5)
            ).astype(BF16)
            key_sum = key_sum + dot_tn(query, grads)
            value_sum = value_sum + dot_tn(up, low)
        lane = ffn + width + h * HD
        acts_ref[0, :, lane : lane + HD] = key_sum.T.astype(BF16)
        lane = lane + width
        acts_ref[0, :, lane : lane + HD] = value_sum.T.astype(BF16)

    part_ref[...] = dot_nt(acts_ref[0], wcat_ref[...])

    channels(chan_ref, tok_ref.at[0], g, count, width, pad)

    @pl.when(step == 0)
    def _():
        tapsum_ref[...] = jnp.zeros(tapsum_ref.shape, F32)

    for start in range(0, length, 128):
        here = start + lax.broadcasted_iota(jnp.int32, (128, 1), 0)
        docs = doc_of(starts_ref, step, here)
        own = [ref[pad + start : pad + start + 128, :] for ref in conv_refs]
        back = jnp.zeros((128, width), F32)
        for shift in range(-3, 4):
            begin = pad + start + shift
            moved = chan_ref[begin : begin + 128, :]
            linked = docs == doc_of(starts_ref, step, here + shift)
            if shift != 0:
                moved = jnp.where(linked, moved, 0.0)
            base = 0
            mixed = jnp.zeros((128, width), F32)
            for k, taps in enumerate(TAPS):
                half = taps // 2
                if abs(shift) <= half:
                    tap = base + shift + half
                    tapsum_ref[tap : tap + 1, :] += jnp.sum(own[k] * moved, axis=0, keepdims=True)
                    tap = base - shift + half
                    mixed = mixed + conv_refs[k][begin : begin + 128, :] * taps_ref[tap : tap + 1, :]
                base += taps
            back = back + (jnp.where(linked, mixed, 0.0) if shift != 0 else mixed)
        for which in range(count):

            @pl.when(g == which)
            def _():
                part_ref[start : start + 128, which * width : (which + 1) * width] += back

    for k, out in enumerate((p0, p1, p2, p3)):
        out[0] = part_ref[pl.ds(pl.multiple_of((g ^ k) * rows, rows), rows), :].astype(BF16)


def block(shape):
    zeros = (0,) * (len(shape) - 1)
    return pl.BlockSpec((1,) + tuple(shape[1:]), lambda i: (i,) + zeros)


def whole(shape):
    zeros = (0,) * len(shape)
    return pl.BlockSpec(tuple(shape), lambda i: zeros)


def smem():
    return pl.BlockSpec(memory_space=pltpu.SMEM)


def struct(shape, dtype):
    return jax.ShapeDtypeStruct(tuple(shape), dtype)


def params():
    return pltpu.CompilerParams(dimension_semantics=("arbitrary",), vmem_limit_bytes=VMEM_LIMIT)


def local(
    groups, count, tokens, cotangent, path_masks, seg_starts, query_weight, key_weight, value_weight, output_weight,
    small_kernel, middle_kernel, large_kernel, small_mixer, middle_mixer, large_mixer, inner_weight, outer_weight,
    norm_gain, norm_bias,
):
    seqs, rows, dim = tokens.shape
    length = rows * count
    width = dim // count
    ffn = inner_weight.shape[1] // count
    wide = ffn + 4 * width
    heads = width // HD
    part = dim // groups
    batch, g = lax.axis_index("batch"), lax.axis_index("seq")
    g_arr = g.astype(jnp.int32).reshape(1)

    def send_seq(value, flip):
        return lax.ppermute(value, "seq", [(i, i ^ flip) for i in range(count)])

    def gather(value):
        far = send_seq(value, 2)
        near = send_seq(value, 1)
        return value, near, far, send_seq(far, 1)

    def columns(weight):
        return lax.dynamic_slice_in_dim(weight, g * (weight.shape[1] // count), weight.shape[1] // count, axis=1)

    def row_slice(weight):
        return lax.dynamic_slice_in_dim(weight, g * (weight.shape[0] // count), weight.shape[0] // count, axis=0)

    token_parts = gather(tokens)
    wqkv = jnp.concatenate([columns(query_weight), columns(key_weight), columns(value_weight)], axis=1)
    win = columns(inner_weight)
    wcat = jnp.concatenate([win, wqkv], axis=1)
    wrow = jnp.concatenate(
        [row_slice(w) for w in (outer_weight, output_weight, small_mixer, middle_mixer, large_mixer)], axis=0
    )
    taps = columns(
        jnp.concatenate([small_kernel, middle_kernel, large_kernel, jnp.zeros((1, dim), BF16)], axis=0)
    ).astype(F32)

    piece = (seqs, rows, dim)
    full = (seqs, length, dim)
    p0, p1, p2, p3, tok_full, mcat, slope, qkv, probs, scaled = pl.pallas_call(
        functools.partial(forward_kernel, count),
        grid=(seqs,),
        in_specs=[smem()] * 3
        + [block(piece)] * 4
        + [whole(wqkv.shape), whole(win.shape), whole(wrow.shape), whole(taps.shape)],
        out_specs=[block(piece)] * 4
        + [
            block(full),
            block((seqs, length, wide)),
            block((seqs, length, ffn)),
            block((seqs, length, 3 * width)),
            block((seqs, heads, length, length)),
            block((seqs, length, width)),
        ],
        out_shape=[struct(piece, BF16)] * 4
        + [
            struct(full, BF16),
            struct((seqs, length, wide), BF16),
            struct((seqs, length, ffn), F32),
            struct((seqs, length, 3 * width), BF16),
            struct((seqs, heads, length, length), BF16),
            struct((seqs, length, width), F32),
        ],
        scratch_shapes=[pltpu.VMEM((length + 16, width), F32), pltpu.VMEM((length, dim), F32)],
        compiler_params=params(),
    )(g_arr, path_masks, seg_starts, *token_parts, wqkv, win, wrow, taps)

    def scatter(a, b, c, d):
        away = send_seq(d, 1)
        near = send_seq(b, 1)
        far = send_seq((c.astype(F32) + away.astype(F32)).astype(BF16), 2)
        return a, near, far

    own, near, far = scatter(p0, p1, p2, p3)
    gain_row = norm_gain.reshape(1, dim)
    bias_row = norm_bias.reshape(1, dim)
    block_output, summed_grad, low_grad, norm_sums = pl.pallas_call(
        norm_kernel,
        grid=(seqs,),
        in_specs=[block(piece)] * 5 + [whole((1, dim))] * 2,
        out_specs=[block(piece)] * 3 + [whole((8, dim))],
        out_shape=[struct(piece, BF16), struct(piece, F32), struct(piece, BF16), struct((8, dim), F32)],
        compiler_params=params(),
    )(tokens, own, near, far, cotangent, gain_row, bias_row)

    low_parts = gather(low_grad)
    i0, i1, i2, i3, acts, tap_sums, low_full = pl.pallas_call(
        functools.partial(backward_kernel, count),
        grid=(seqs,),
        in_specs=[smem()] * 3
        + [block(piece)] * 4
        + [
            block(full),
            block((seqs, length, ffn)),
            block((seqs, length, 3 * width)),
            block((seqs, heads, length, length)),
            block((seqs, length, width)),
            whole(wrow.shape),
            whole(wcat.shape),
            whole(taps.shape),
        ],
        out_specs=[block(piece)] * 4 + [block((seqs, length, ffn + 3 * width)), whole(taps.shape), block(full)],
        out_shape=[struct(piece, BF16)] * 4
        + [struct((seqs, length, ffn + 3 * width), BF16), struct(taps.shape, F32), struct(full, BF16)],
        scratch_shapes=[pltpu.VMEM((length, width), BF16)]
        + [pltpu.VMEM((length + 16, width), F32)] * 4
        + [pltpu.VMEM((length, dim), F32)],
        compiler_params=params(),
    )(g_arr, path_masks, seg_starts, *low_parts, tok_full, slope, qkv, probs, scaled, wrow, wcat, taps)

    own, near, far = scatter(i0, i1, i2, i3)
    input_grad = (summed_grad + (own.astype(F32) + near.astype(F32) + far.astype(F32))).astype(BF16)

    all_rows = seqs * length
    low_rows = low_full.reshape(all_rows, dim)
    mcat_rows = mcat.reshape(all_rows, wide)
    outer_sum = dot_tn(mcat_rows[:, 0:ffn], low_rows)
    branch_sum = dot_tn(mcat_rows[:, ffn:], low_rows)
    tok_rows = tok_full.reshape(all_rows, dim)
    act_rows = acts.reshape(all_rows, ffn + 3 * width)
    inner_sum = dot_tn(tok_rows, act_rows[:, 0:ffn])
    qkv_sum = dot_tn(tok_rows, act_rows[:, ffn:])
    tap_rows = tap_sums.shape[0] - 1
    tap_cols = lax.dynamic_update_slice_in_dim(
        jnp.zeros((dim, tap_rows), F32), tap_sums[0:tap_rows].T, g * width, axis=0
    )
    op_counts = jnp.sum(path_masks, axis=0).astype(F32) * (g == 0).astype(F32)
    extra = jnp.concatenate(
        [tap_cols, norm_sums[0:2].T, jnp.broadcast_to(op_counts[None, :], (dim, op_counts.shape[0]))], axis=1
    )
    qkv_sum = jnp.concatenate([qkv_sum, extra], axis=1)

    bits = groups.bit_length() - 1
    top = count.bit_length() - 1

    def halve(value, bit):
        pre, blocks, r, w = value.shape
        split = value.reshape(pre, blocks // 2, 2, r, w)
        mine = (batch >> bit) & 1
        sent = lax.dynamic_index_in_dim(split, 1 - mine, axis=2, keepdims=False).astype(BF16)
        kept = lax.dynamic_index_in_dim(split, mine, axis=2, keepdims=False).astype(F32)
        got = lax.ppermute(sent, "batch", [(i, i ^ (1 << bit)) for i in range(groups)])
        return kept + got.astype(F32)

    def reduce_columns(value):
        value = value.reshape(1, groups, part, value.shape[1])
        for bit in range(bits):
            value = halve(value, bit)
        low = value[0, 0].astype(BF16)
        return jnp.stack(gather(low))

    def pairs(want):
        found = []
        for b in range(groups):
            for s in range(count):
                to = want(b, s)
                if to is not None:
                    found.append((b * count + s, to[0] * count + to[1]))
        return found

    def lead(b):
        return b >> (bits - top)

    def reduce_rows(value, pre):
        blocks = groups // count
        value = value.reshape(pre, blocks, value.shape[0] // (pre * blocks), value.shape[1])
        for bit in range(bits - top):
            value = halve(value, bit)
        for bit in range(top):
            level = bits - top + bit

            def target(b, s, bit=bit, level=level):
                settled = (lead(b) ^ s) & ((1 << bit) - 1)
                if settled or not ((lead(b) ^ s) >> bit) & 1:
                    return None
                return b ^ (1 << level), s

            got = lax.ppermute(value.astype(BF16), ("batch", "seq"), pairs(target))
            value = value + got.astype(F32)
        low = jnp.where(lead(batch) == g, value, 0.0).astype(BF16)
        low = low + lax.ppermute(
            low, ("batch", "seq"), pairs(lambda b, s: (b, s ^ 2) if s == lead(b) else None)
        )
        low = low + lax.ppermute(
            low, ("batch", "seq"), pairs(lambda b, s: (b, s ^ 1) if (s ^ lead(b)) & 1 == 0 else None)
        )
        return low[:, 0]

    outer_low = reduce_rows(outer_sum, 1)
    branch_low = reduce_rows(branch_sum, 4)
    inner_low = reduce_columns(inner_sum)
    qkv_low = reduce_columns(qkv_sum)

    def ordered(stack):
        return [lax.dynamic_index_in_dim(stack, g ^ k, axis=0, keepdims=False).astype(F32) for k in range(count)]

    inner_parts = ordered(inner_low)
    qkv_parts = ordered(qkv_low)
    extras = sum(p[:, 3 * width :] for p in qkv_parts)
    counts = extras[0, tap_rows + 2 :]
    query_grad, key_grad, value_grad = [
        jnp.concatenate([p[:, i * width : (i + 1) * width] for p in qkv_parts], axis=1) / counts[0] for i in range(3)
    ]
    inner_grad = jnp.concatenate(inner_parts, axis=1) / counts[4]
    outer_grad = outer_low[0].astype(F32) / counts[4]
    branch_f = branch_low.astype(F32)
    bounds = [0]
    for taps_k in TAPS:
        bounds.append(bounds[-1] + taps_k)
    kernel_grads = [(extras[:, bounds[k] : bounds[k + 1]] / counts[k + 1]).T for k in range(3)]
    return (
        block_output,
        input_grad,
        query_grad,
        key_grad,
        value_grad,
        branch_f[0] / counts[0],
        kernel_grads[0],
        kernel_grads[1],
        kernel_grads[2],
        branch_f[1] / counts[1],
        branch_f[2] / counts[2],
        branch_f[3] / counts[3],
        inner_grad,
        outer_grad,
        extras[:, tap_rows],
        extras[:, tap_rows + 1],
    )


def solution(mesh):
    rows = P("batch", "seq", None)
    groups = P("batch", None)
    in_specs = (rows, rows, groups, groups) + (P(),) * 14
    out_specs = (
        (rows, rows)
        + (groups,) * 4
        + (P(None, "batch"),) * 3
        + (groups,) * 5
        + (P("batch"), P("batch"))
    )
    body = functools.partial(local, mesh.shape["batch"], mesh.shape["seq"])
    return jax.shard_map(body, mesh=mesh, in_specs=in_specs, out_specs=out_specs, check_vma=False)
```

```python
import functools

import jax
import jax.numpy as jnp
from jax import lax
from jax.experimental import pallas as pl
from jax.experimental.pallas import tpu as pltpu
from jax.sharding import PartitionSpec as P

HD = 64
ORDER = "OBRTCSUDobIQVobiqoibqiobiqobqiq"
PREPARE, FORWARD, BACKWARD, PRODUCT = 6, 8, 10, 8
EPSILON = 1e-05
MASKED = -1e30
TAPS = (3, 5, 7)
F32 = jnp.float32
BF16 = jnp.bfloat16


def dot_nn(left, right):
    return jnp.dot(left, right, preferred_element_type=F32)


def dot_nt(left, right):
    return lax.dot_general(left, right, (((1,), (1,)), ((), ())), preferred_element_type=F32)


def dot_tn(left, right):
    return lax.dot_general(left, right, (((0,), (0,)), ((), ())), preferred_element_type=F32)


def doc_of(starts_ref, row, positions):
    found = jnp.zeros(positions.shape, jnp.int32)
    for which in range(starts_ref.shape[1]):
        found = found + (starts_ref[row, which] <= positions).astype(jnp.int32)
    return found


def assemble(full_ref, pieces, g):
    for k, piece in enumerate(pieces):
        rows = piece.shape[0]
        full_ref[pl.ds(pl.multiple_of((g ^ k) * rows, rows), rows), :] = piece[...]


def spread(part_ref, outs, g):
    for k, out in enumerate(outs):
        rows = out.shape[0]
        out[...] = part_ref[pl.ds(pl.multiple_of((g ^ k) * rows, rows), rows), :].astype(out.dtype)


def channels(out_ref, source, g, count, width, pad):
    length = source.shape[0]
    out_ref[0:pad, :] = jnp.zeros((pad, width), F32)
    out_ref[pad + length : 2 * pad + length, :] = jnp.zeros((pad, width), F32)
    for which in range(count):

        @pl.when(g == which)
        def _():
            out_ref[pad : pad + length, :] = source[:, which * width : (which + 1) * width].astype(F32)


def prepare_kernel(
    count, place_in, query_ref, key_ref, value_ref, inner_ref, outer_ref, output_ref, m3_ref, m5_ref, m7_ref,
    tok_in, cot_in, k3_ref, k5_ref, k7_ref, gain_ref, bias_ref, wcat_ref, wrow_ref, taps_ref, rows_ref, tok_ref, cot_ref, place_ref, buf_ref, sems,
):
    g = place_in[0]
    unit = g ^ (count // 2)
    for i in range(place_ref.shape[0]):
        place_ref[i] = place_in[i]
    dim, ffn = inner_ref.shape[0], inner_ref.shape[1] // count
    width = dim // count
    copies = [
        pltpu.make_async_copy(ref, buf_ref.at[i], sems.at[i]) for i, ref in enumerate((query_ref, key_ref, value_ref))
    ]
    copies.append(
        pltpu.make_async_copy(
            inner_ref.at[:, pl.ds(pl.multiple_of(unit * ffn, ffn), ffn)], wcat_ref.at[:, pl.ds(0, ffn)], sems.at[3]
        )
    )
    copies.append(
        pltpu.make_async_copy(
            outer_ref.at[pl.ds(pl.multiple_of(unit * ffn, ffn), ffn)], wrow_ref.at[pl.ds(0, ffn)], sems.at[4]
        )
    )
    for i, ref in enumerate((output_ref, m3_ref, m5_ref, m7_ref)):
        copies.append(
            pltpu.make_async_copy(
                ref.at[pl.ds(pl.multiple_of(g * width, width), width)],
                wrow_ref.at[pl.ds(ffn + i * width, width)],
                sems.at[5 + i],
            )
        )
    copies.append(pltpu.make_async_copy(tok_in, tok_ref, sems.at[9]))
    copies.append(pltpu.make_async_copy(cot_in, cot_ref, sems.at[10]))
    for copy in copies:
        copy.start()

    rows_ref[...] = jnp.zeros(rows_ref.shape, F32)
    rows_ref[0:1, :] = gain_ref[...].astype(F32).reshape(1, dim)
    rows_ref[1:2, :] = bias_ref[...].astype(F32).reshape(1, dim)
    taps_ref[...] = jnp.zeros(taps_ref.shape, F32)
    for which in range(count):

        @pl.when(g == which)
        def _(which=which):
            at = 0
            for ref in (k3_ref, k5_ref, k7_ref):
                taps = ref[:, which * width : (which + 1) * width].astype(F32)
                taps_ref[at : at + ref.shape[0], :] = taps
                at += ref.shape[0]

    for i in range(3):
        copies[i].wait()
        for which in range(count):

            @pl.when(g == which)
            def _(i=i, which=which):
                wcat_ref[:, ffn + i * width : ffn + (i + 1) * width] = buf_ref[
                    i, :, which * width : (which + 1) * width
                ]

    for copy in copies[3:]:
        copy.wait()


def forward_kernel(
    count, which, g_ref, masks_ref, starts_ref, t0, t1, t2, t3, wcat_ref, wrow_ref, taps_ref,
    p0, p1, p2, p3, tok_ref, mcat_ref, slope_ref, qkv_ref, probs_ref, scaled_ref,
    chan_ref, part_ref,
):
    g = g_ref[0]
    assemble(tok_ref, (t0.at[which], t1, t2, t3), g)
    length, ffn = slope_ref.shape
    width = scaled_ref.shape[1]
    heads = width // HD
    masks = [masks_ref[which, c].astype(F32) for c in range(5)]

    used = [masks_ref[which, c] > 0 for c in range(5)]
    convolved = masks_ref[which, 1] + masks_ref[which, 2] + masks_ref[which, 3] > 0

    @pl.when(used[0])
    def _():
        qkv = dot_nn(tok_ref[...], wcat_ref[:, ffn:]).astype(BF16)
        qkv_ref[:, 0:width] = qkv[:, 0:width] * jnp.asarray(HD**-0.5, BF16)
        qkv_ref[:, width:] = qkv[:, width:]

        linked = doc_of(starts_ref, which, lax.broadcasted_iota(jnp.int32, (length, 1), 0)) == doc_of(
            starts_ref, which, lax.broadcasted_iota(jnp.int32, (1, length), 1)
        )
        ones = jnp.ones((length, HD), BF16)
        for h in range(heads):
            keys = qkv_ref[:, width + h * HD : width + (h + 1) * HD]
            values = jnp.concatenate([qkv_ref[:, 2 * width + h * HD : 2 * width + (h + 1) * HD], ones], axis=1)
            scores = jnp.where(linked, dot_nt(qkv_ref[:, h * HD : (h + 1) * HD], keys), MASKED)
            weights = jnp.exp(scores - jnp.max(scores, axis=1, keepdims=True))
            low = (weights * (1.0 / jnp.sum(weights, axis=1, keepdims=True))).astype(BF16)
            probs_ref[h] = low
            both = dot_nn(low, values)
            attended = both[:, 0:HD]
            scaled_ref[:, h * HD : (h + 1) * HD] = attended / both[:, HD : 2 * HD]
            mcat_ref[:, ffn + h * HD : ffn + (h + 1) * HD] = attended.astype(BF16) * masks[0].astype(BF16)

    @pl.when(jnp.logical_not(used[0]))
    def _():
        mcat_ref[:, ffn : ffn + width] = jnp.zeros((length, width), BF16)
        for ref in (qkv_ref, probs_ref, scaled_ref):
            ref[...] = jnp.zeros(ref.shape, ref.dtype)

    @pl.when(convolved)
    def _():
        pad = 8
        channels(chan_ref, tok_ref, g, count, width, pad)
        tile = min(length, 128)
        for start in range(0, length, tile):
            sums = [jnp.zeros((tile, width), F32) for _ in TAPS]
            here = start + lax.broadcasted_iota(jnp.int32, (tile, 1), 0)
            docs = doc_of(starts_ref, which, here)
            for shift in range(-3, 4):
                moved = chan_ref[pad + start + shift : pad + start + shift + tile, :]
                if shift != 0:
                    moved = jnp.where(docs == doc_of(starts_ref, which, here + shift), moved, 0.0)
                base = 0
                for k, taps in enumerate(TAPS):
                    if abs(shift) <= taps // 2:
                        tap = base + shift + taps // 2
                        sums[k] = sums[k] + moved * taps_ref[tap : tap + 1, :]
                    base += taps
            for k in range(3):
                lane = ffn + (k + 1) * width
                mcat_ref[start : start + tile, lane : lane + width] = (sums[k] * masks[k + 1]).astype(BF16)

    @pl.when(jnp.logical_not(convolved))
    def _():
        mcat_ref[:, ffn + width :] = jnp.zeros((length, 3 * width), BF16)

    @pl.when(used[4])
    def _():
        tile = min(length, 256)
        for start in range(0, length, tile):
            hidden = dot_nn(tok_ref[start : start + tile, :], wcat_ref[:, 0:ffn])
            cdf = 0.5 + 0.5 * lax.erf(hidden * (0.5**0.5))
            density = jnp.exp(-0.5 * hidden * hidden) * 0.3989422804014327
            mcat_ref[start : start + tile, 0:ffn] = (hidden * cdf * masks[4]).astype(BF16)
            slope_ref[start : start + tile, :] = (cdf + hidden * density).astype(slope_ref.dtype)

    @pl.when(jnp.logical_not(used[4]))
    def _():
        mcat_ref[:, 0:ffn] = jnp.zeros((length, ffn), BF16)
        slope_ref[...] = jnp.zeros(slope_ref.shape, slope_ref.dtype)

    part_ref[...] = dot_nn(mcat_ref[...], wrow_ref[...])
    spread(part_ref, (p0, p1, p2, p3), g)


def norm_kernel(which, *refs):
    kept_ref, far_ref, rows_ref, tok_ref, cot_ref = refs[:5]
    out_all, grad_ref, low_ref, sums_ref, out_ref, sem = refs[-6:]
    summed = tok_ref[which].astype(F32) + (kept_ref[...] + far_ref[...].astype(F32))
    centred = summed - jnp.mean(summed, axis=1, keepdims=True)
    inverse = lax.rsqrt(jnp.mean(centred * centred, axis=1, keepdims=True) + EPSILON)
    normed = centred * inverse
    gain = rows_ref[0:1, :]
    out_ref[...] = (normed * gain + rows_ref[1:2, :]).astype(BF16)
    out_copy = pltpu.make_async_copy(out_ref, out_all.at[which], sem)
    out_copy.start()
    upstream = cot_ref[which].astype(F32)
    sums_ref[...] = jnp.zeros(sums_ref.shape, F32)
    sums_ref[0:1, :] = jnp.sum(upstream * normed, axis=0, keepdims=True)
    sums_ref[1:2, :] = jnp.sum(upstream, axis=0, keepdims=True)
    scaled = upstream * gain
    grad = inverse * (
        scaled
        - jnp.mean(scaled, axis=1, keepdims=True)
        - normed * jnp.mean(scaled * normed, axis=1, keepdims=True)
    )
    grad_ref[...] = grad
    low_ref[...] = grad.astype(BF16)
    out_copy.wait()


def cross_kernel(*refs):
    leaving, away, own, near = refs[:4]
    crossing_ref, kept_ref = refs[-2:]
    crossing_ref[...] = (leaving[...].astype(F32) + away[...].astype(F32)).astype(BF16)
    kept = own[...].astype(F32) + near[...].astype(F32)
    if len(refs) == 7:
        kept = kept + refs[4][...]
    kept_ref[...] = kept


def backward_kernel(
    count, which, g_ref, masks_ref, starts_ref, low_ref, tok_ref, slope_ref, qkv_ref, probs_ref, scaled_ref,
    wcat_ref, wrow_ref, taps_ref,
    p0, p1, p2, p3, acts_ref, tapsum_ref,
    up_ref, chan_ref, c3_ref, c5_ref, c7_ref, part_ref,
):
    g = g_ref[0]
    length, ffn = slope_ref.shape
    width = scaled_ref.shape[1]
    heads = width // HD
    pad = 8
    masks = [masks_ref[which, c].astype(F32) for c in range(5)]

    ups = dot_nt(low_ref[...], wrow_ref[ffn:, :])
    up_ref[...] = (ups[:, 0:width] * masks[0]).astype(BF16)
    conv_refs = (c3_ref, c5_ref, c7_ref)
    for k, ref in enumerate(conv_refs):
        ref[0:pad, :] = jnp.zeros((pad, width), F32)
        ref[pad + length : 2 * pad + length, :] = jnp.zeros((pad, width), F32)
        ref[pad : pad + length, :] = (
            (ups[:, (k + 1) * width : (k + 2) * width] * masks[k + 1]).astype(BF16).astype(F32)
        )

    tile = min(length, 256)
    for start in range(0, length, tile):
        grads = dot_nt(low_ref[start : start + tile, :], wrow_ref[0:ffn, :])
        grads = (grads * masks[4]).astype(BF16).astype(F32)
        acts_ref[start : start + tile, 0:ffn] = (grads * slope_ref[start : start + tile, :].astype(F32)).astype(BF16)

    for h in range(heads):
        keys = qkv_ref[:, width + h * HD : width + (h + 1) * HD]
        values = qkv_ref[:, 2 * width + h * HD : 2 * width + (h + 1) * HD]
        query = qkv_ref[:, h * HD : (h + 1) * HD]
        up = up_ref[:, h * HD : (h + 1) * HD]
        low = probs_ref[h]
        shared = jnp.sum(up.astype(F32) * scaled_ref[:, h * HD : (h + 1) * HD], axis=1, keepdims=True)
        grads = (low.astype(F32) * (dot_nt(up, values) - shared)).astype(BF16)
        lane = ffn + h * HD
        acts_ref[:, lane : lane + HD] = (dot_nn(grads, keys) * (HD**-0.5)).astype(BF16)
        acts_ref[:, lane + width : lane + width + HD] = dot_tn(query, grads).T.astype(BF16)
        acts_ref[:, lane + 2 * width : lane + 2 * width + HD] = dot_tn(up, low).T.astype(BF16)

    part_ref[...] = dot_nt(acts_ref[...], wcat_ref[...])

    tapsum_ref[...] = jnp.zeros(tapsum_ref.shape, F32)

    channels(chan_ref, tok_ref, g, count, width, pad)
    tile = min(length, 128)
    for start in range(0, length, tile):
        here = start + lax.broadcasted_iota(jnp.int32, (tile, 1), 0)
        docs = doc_of(starts_ref, which, here)
        own = [ref[pad + start : pad + start + tile, :] for ref in conv_refs]
        back = jnp.zeros((tile, width), F32)
        for shift in range(-3, 4):
            begin = pad + start + shift
            moved = chan_ref[begin : begin + tile, :]
            linked = docs == doc_of(starts_ref, which, here + shift)
            if shift != 0:
                moved = jnp.where(linked, moved, 0.0)
            base = 0
            mixed = jnp.zeros((tile, width), F32)
            for k, taps in enumerate(TAPS):
                half = taps // 2
                if abs(shift) <= half:
                    tap = base + shift + half
                    tapsum_ref[tap : tap + 1, :] += jnp.sum(own[k] * moved, axis=0, keepdims=True)
                    tap = base - shift + half
                    mixed = mixed + conv_refs[k][begin : begin + tile, :] * taps_ref[tap : tap + 1, :]
                base += taps
            back = back + (jnp.where(linked, mixed, 0.0) if shift != 0 else mixed)
        for member in range(count):

            @pl.when(g == member)
            def _(member=member, back=back):
                part_ref[start : start + tile, member * width : (member + 1) * width] += back

    spread(part_ref, (p0, p1, p2, p3), g)


def join_kernel(place_ref, a, b, c, d, out_ref):
    assemble(out_ref, (a, b, c, d), place_ref[0])


def product_kernel(pairs, take, column, split, bit, spare, ride, begun, g_ref, masks_ref, *refs):
    refs = list(refs)
    lefts, rights, refs = refs[:pairs], refs[pairs : 2 * pairs], refs[2 * pairs :]
    before, refs = (refs[:1], refs[1:]) if begun else ([], refs)
    tapsums, norms, refs = (refs[:pairs], refs[pairs : 2 * pairs], refs[2 * pairs :]) if spare else ([], [], refs)
    if split is None:
        outs, acc_ref = [], refs[0]
    else:
        outs, acc_ref = refs[:2], refs[2]
    g = g_ref[0]
    wide = acc_ref.shape[1] - spare
    for i in range(pairs):
        term = dot_tn(lefts[i][:, take[0] : take[1]], rights[i][:, column[0] : column[1]])
        if i > 0:
            acc_ref[:, 0:wide] += term
        elif begun:
            acc_ref[:, 0:wide] = before[0][...] + term
        else:
            acc_ref[:, 0:wide] = term
    if spare:
        acc_ref[:, wide:] = jnp.zeros((acc_ref.shape[0], spare), F32)
        taps = sum(ref[...] for ref in tapsums).T
        here = pl.ds(pl.multiple_of(g * taps.shape[0], 8), taps.shape[0])
        acc_ref[here, wide : wide + taps.shape[1]] = taps
        norm = sum(ref[...] for ref in norms).T
        acc_ref[:, wide + taps.shape[1] : wide + taps.shape[1] + norm.shape[1]] = norm
    if split is None:
        return
    sent_ref, kept_ref = outs
    mine = (g_ref[1] >> bit) & 1
    if ride:
        lane = lax.broadcasted_iota(jnp.int32, (ride, wide), 1)
        users = jnp.zeros((ride, wide), F32)
        for c in range(masks_ref.shape[1]):
            number = sum(masks_ref[s, c] for s in range(masks_ref.shape[0])).astype(F32)
            users = jnp.where(lane == c, number, users)
        sent_ref[sent_ref.shape[0] - ride :, :] = users.astype(BF16)
        kept_ref[sent_ref.shape[0] - ride :, :] = users
    for j in range((sent_ref.shape[0] - ride) // split):
        start = 2 * j * split
        there = pl.ds(pl.multiple_of(start + (1 - mine) * split, 16), split)
        here = pl.ds(pl.multiple_of(start + mine * split, 16), split)
        sent_ref[j * split : (j + 1) * split, :] = acc_ref[there, :].astype(BF16)
        kept_ref[j * split : (j + 1) * split, :] = acc_ref[here, :]


def step_kernel(block, bit, place_ref, got_ref, kept_ref, sent_ref, rest_ref):
    mine = (place_ref[1] >> bit) & 1
    for j in range(sent_ref.shape[0] // block):
        start = 2 * j * block
        there = pl.ds(pl.multiple_of(start + (1 - mine) * block, 16), block)
        here = pl.ds(pl.multiple_of(start + mine * block, 16), block)
        sent_ref[j * block : (j + 1) * block, :] = (kept_ref[there, :] + got_ref[there, :].astype(F32)).astype(BF16)
        rest_ref[j * block : (j + 1) * block, :] = kept_ref[here, :] + got_ref[here, :].astype(F32)


def add_kernel(got_ref, kept_ref, sum_ref, low_ref):
    total = kept_ref[...] + got_ref[...].astype(F32)
    sum_ref[...] = total
    low_ref[...] = total.astype(BF16)


def own_kernel(which, place_ref, got_ref, kept_ref, low_ref):
    low_ref[...] = jnp.where(place_ref[which] == 1, kept_ref[...] + got_ref[...].astype(F32), 0.0).astype(BF16)


def both_kernel(left_ref, right_ref, out_ref):
    out_ref[...] = (left_ref[...].astype(F32) + right_ref[...].astype(F32)).astype(out_ref.dtype)


def rows_kernel(columns, ride, left_ref, right_ref, *refs):
    outs = refs[len(refs) - len(columns) - (1 if ride else 0) :]
    if ride:
        behind = slice(left_ref.shape[0] - ride, left_ref.shape[0])
        counts = (left_ref[behind, :].astype(F32) + right_ref[behind, :].astype(F32))[0:8, 0:128]
        outs[-1][...] = counts
    else:
        counts = refs[0][...]
    at = 0
    for column, out in zip(columns, outs):
        rows = slice(at, at + out.shape[0])
        total = left_ref[rows, :].astype(F32) + right_ref[rows, :].astype(F32)
        out[...] = total / counts[0:1, column : column + 1]
        at += out.shape[0]


def inner_kernel(g_ref, d, counts_ref, a, b, c, out_ref):
    for k, piece in enumerate((a, b, c, d)):
        lanes = piece.shape[1]
        start = pl.multiple_of((g_ref[0] ^ k ^ 2) * lanes, lanes)
        out_ref[:, pl.ds(start, lanes)] = piece[...].astype(F32) / counts_ref[0:1, 4:5]


def qkv_kernel(g_ref, d, counts_ref, a, b, c, query_ref, key_ref, value_ref, *refs):
    *smalls, gain_out, bias_out, buf_ref = refs
    norm_outs = (gain_out, bias_out)
    pieces = (a, b, c, d)
    for k, piece in enumerate(pieces):
        buf_ref[g_ref[0] ^ k] = piece[...].astype(F32)
    width = query_ref.shape[1] // len(pieces)
    for i, out in enumerate((query_ref, key_ref, value_ref)):
        for m in range(len(pieces)):
            out[:, m * width : (m + 1) * width] = buf_ref[m, :, i * width : (i + 1) * width] / counts_ref[0:1, 0:1]
    spare = sum(buf_ref[m, :, 3 * width :] for m in range(len(pieces))).T
    at = 0
    for i, out in enumerate(smalls):
        out[...] = spare[at : at + out.shape[0], :] / counts_ref[0:1, i + 1 : i + 2]
        at += out.shape[0]
    for i, out in enumerate(norm_outs):
        out[...] = spare[at + 1 + i : at + 2 + i, :].reshape(out.shape)


def total_kernel(which, *refs):
    far_ref, kept_ref = refs[:2]
    out_all, out_ref, sem = refs[-3:]
    out_ref[...] = (kept_ref[...] + far_ref[...].astype(F32)).astype(BF16)
    copy = pltpu.make_async_copy(out_ref, out_all.at[which], sem)
    copy.start()
    copy.wait()


def smem():
    return pl.BlockSpec(memory_space=pltpu.SMEM)


def struct(shape, dtype):
    return jax.ShapeDtypeStruct(tuple(shape), dtype)


def scratch_of(shape):
    return pltpu.VMEM(shape.shape, shape.dtype)


def local(
    groups, count, tokens, cotangent, path_masks, seg_starts, query_weight, key_weight, value_weight, output_weight,
    small_kernel, middle_kernel, large_kernel, small_mixer, middle_mixer, large_mixer, inner_weight, outer_weight,
    norm_gain, norm_bias,
):
    seqs, rows, dim = tokens.shape
    length = rows * count
    width = dim // count
    ffn = inner_weight.shape[1] // count
    wide = ffn + 4 * width
    act = ffn + 3 * width
    heads = width // HD
    part = dim // groups
    outer_part = part * ffn // width
    bits = groups.bit_length() - 1
    top = count.bit_length() - 1
    batch, g = lax.axis_index("batch").astype(jnp.int32), lax.axis_index("seq").astype(jnp.int32)
    owner = batch >> (bits - top)
    place = jnp.stack([g, batch, (owner == g).astype(jnp.int32), (owner == g ^ (count // 2)).astype(jnp.int32)])

    turn = []

    def call(kernel, arrays, scalars, out_shape, limit, scratch=(), ins="", outs="", aliases=()):
        ins = ins + "v" * (len(arrays) - len(ins))
        outs = outs + "v" * (len(out_shape) - len(outs))
        before = len(scalars) + len(arrays)
        behind = list(turn)

        def body(*refs):
            kernel(*refs[:before], *refs[before + len(behind) :])

        def seen(kinds):
            spaces = {"h": pltpu.HBM, "s": pltpu.SMEM}
            return [pl.BlockSpec(memory_space=spaces.get(kind, pltpu.VMEM)) for kind in kinds]

        def home(kind):
            return pltpu.VMEM if kind == "v" else pltpu.HBM

        def lies(x, kind):
            return pltpu.with_memory_space_constraint(x, home(kind))

        out = pl.pallas_call(
            body,
            in_specs=[smem()] * len(scalars) + seen(ins) + [pl.BlockSpec(memory_space=pl.ANY)] * len(behind),
            out_specs=seen(outs),
            out_shape=[home(kind)(x.shape, x.dtype) for kind, x in zip(outs, out_shape)],
            scratch_shapes=list(scratch),
            input_output_aliases={len(scalars) + i: o for i, o in aliases},
            compiler_params=pltpu.CompilerParams(vmem_limit_bytes=limit * 1024 * 1024),
            cost_estimate=pl.CostEstimate(flops=1000, bytes_accessed=1000, transcendentals=0),
        )(
            *[lies(x, "h") for x in scalars],
            *[lies(x, kind) for x, kind in zip(arrays, ins)],
            *[lies(x, kind) for x, kind in behind],
        )
        smallest = min((i for i in range(len(out)) if outs[i] != "s"), key=lambda i: out[i].size)
        turn[:] = [(out[smallest], outs[smallest])]
        return out

    def hold(value):
        return call(lambda *refs: None, [value], [], [struct(value.shape, value.dtype)], 1, aliases=[(0, 0)])[0]

    turned = []

    def listed(found):
        turned.append(None)
        at = len(turned) % len(found)
        return found[at:] + found[:at]

    def send_seq(value, flip):
        return lax.ppermute(value, "seq", listed([(i, i ^ flip) for i in range(count)]))

    def exchange(sent, bit):
        return lax.ppermute(sent, "batch", listed([(i, i ^ (1 << bit)) for i in range(groups)]))

    def lead(b):
        return b >> (bits - top)

    def pairs(want):
        found = []
        for b in range(groups):
            for s in range(count):
                to = want(b, s)
                if to is not None:
                    found.append((b * count + s, to[0] * count + to[1]))
        return listed(found)

    piece = struct((rows, dim), BF16)
    full = struct((length, dim), BF16)
    pads = pltpu.VMEM((length + 16, width), F32)

    token_near = [send_seq(tokens[s], 1) for s in range(seqs)]
    token_far = [send_seq(tokens[s], 2) for s in range(seqs)]
    tap_rows = sum(TAPS) + 1
    wcat, wrow, taps, norm_rows, tokens_here, cotangent_here, place = call(
        functools.partial(prepare_kernel, count),
        [
            query_weight, key_weight, value_weight, inner_weight, outer_weight, output_weight, small_mixer,
            middle_mixer, large_mixer, tokens, cotangent, small_kernel, middle_kernel, large_kernel, norm_gain, norm_bias,
        ],
        [place],
        [
            struct((dim, act), BF16), struct((wide, dim), BF16), struct((tap_rows, width), F32), struct((8, dim), F32),
            struct(tokens.shape, BF16), struct(tokens.shape, BF16), struct(place.shape, jnp.int32),
        ],
        PREPARE,
        [pltpu.VMEM((3, dim, dim), BF16), pltpu.SemaphoreType.DMA((11,))],
        "h" * 11 + "w" * 5,
        "vvvvvvs",
    )

    saved_shapes = [
        full,
        struct((length, wide), BF16),
        struct((length, ffn), BF16),
        struct((length, 3 * width), BF16),
        struct((heads, length, length), BF16),
        struct((length, width), F32),
    ]

    def forward(s, parts):
        p0, p1, p2, p3, *kept = call(
            functools.partial(forward_kernel, count, s),
            [tokens_here, *parts, wcat, wrow, taps],
            [place, path_masks, seg_starts],
            [piece] * 4 + saved_shapes,
            FORWARD,
            [pads, pltpu.VMEM((length, dim), F32)],
        )
        return (p2, send_seq(p3, 1), p0, send_seq(p1, 1)), kept

    def cross(terms, grad=None):
        more = [] if grad is None else [grad]
        crossing, kept = call(
            cross_kernel, [*terms, *more], [], [piece, struct((rows, dim), F32)], 4
        )
        return kept, send_seq(crossing, 2)

    def normalise(s, kept, far, outputs):
        return call(
            functools.partial(norm_kernel, s),
            [kept, far, norm_rows, tokens_here, cotangent_here, *outputs],
            [],
            [struct((seqs, rows, dim), BF16), struct((rows, dim), F32), piece, struct((8, dim), F32)],
            4,
            [scratch_of(piece), pltpu.SemaphoreType.DMA],
            "vvvvvh"[: 5 + len(outputs)],
            "hvvv",
            [(5, 0)] if outputs else [],
        )

    def join(s):
        (whole,) = call(join_kernel, lows[s], [place], [full], 4)
        joined.append(whole)

    def backward(s, low_full, kept):
        tok_full, _, slope, qkv, probs, scaled = kept
        p0, p1, p2, p3, acts, taps_sum = call(
            functools.partial(backward_kernel, count, s),
            [low_full, tok_full, slope, qkv, probs, scaled, wcat, wrow, taps],
            [place, path_masks, seg_starts],
            [piece] * 4 + [struct((length, act), BF16), struct(taps.shape, F32)],
            BACKWARD,
            [pltpu.VMEM((length, width), BF16)] + [pads] * 4 + [pltpu.VMEM((length, dim), F32)],
        )
        return (p2, send_seq(p3, 1), p0, send_seq(p1, 1)), acts, taps_sum

    def product(lefts, rights, take, column, block=None, bit=0, beside=(), ride=0, begun=()):
        m, w = take[1] - take[0], column[1] - column[0]
        spare = -w % 128 if beside else 0
        split = block if block and block % 16 == 0 else None
        acc = struct((m, w + spare), F32)
        shapes = [acc] if split is None else [struct((m // 2 + ride, w + spare), BF16), struct((m // 2 + ride, w + spare), F32)]
        out = call(
            functools.partial(product_kernel, len(lefts), take, column, split, bit, spare, ride, len(begun)),
            [*lefts, *rights, *begun, *beside],
            [place, path_masks],
            shapes,
            PRODUCT,
            [] if split is None else [scratch_of(acc)],
        )
        if split is not None or not block:
            return out
        return halves(out[0], bit, block)

    def halves(value, bit, block):
        m, w = value.shape
        split = value.reshape(m // (2 * block), 2, block, w)
        mine = (batch >> bit) & 1
        sent = lax.dynamic_index_in_dim(split, 1 - mine, axis=1, keepdims=False)
        kept = lax.dynamic_index_in_dim(split, mine, axis=1, keepdims=False)
        return sent.reshape(m // 2, w).astype(BF16), kept.reshape(m // 2, w)

    def step(kept, got, bit, block):
        m, w = kept.shape
        if block % 16 != 0:
            return halves(kept + got.astype(F32), bit, block)
        return call(
            functools.partial(step_kernel, block, bit),
            [got, kept],
            [place],
            [struct((m // 2, w), BF16), struct((m // 2, w), F32)],
            4,
        )

    def reduce_rows(sent, kept, block, columns, flip, ride=0):
        got = exchange(sent, 0)
        yield
        for bit in range(1, bits - top):
            sent, kept = step(kept, got, bit, block)
            got = exchange(sent, bit)
            yield
        for bit in range(top):
            level = bits - top + bit

            def target(b, s, bit=bit, level=level):
                settled = (lead(b) ^ s ^ flip) & ((1 << bit) - 1)
                if settled or not ((lead(b) ^ s ^ flip) >> bit) & 1:
                    return None
                return b ^ (1 << level), s

            kept, sent = call(add_kernel, [got, kept], [], [struct(kept.shape, F32), struct(kept.shape, BF16)], 4)
            got = lax.ppermute(sent, ("batch", "seq"), pairs(target))
            yield
        (low,) = call(functools.partial(own_kernel, 3 if flip else 2), [got, kept], [place], [struct(kept.shape, BF16)], 4)
        far = lax.ppermute(low, ("batch", "seq"), pairs(lambda b, s: (b, s ^ 2) if s == lead(b) ^ flip else None))
        yield
        (low,) = call(both_kernel, [far, low], [], [struct(kept.shape, BF16)], 4)
        near = lax.ppermute(
            low, ("batch", "seq"), pairs(lambda b, s: (b, s ^ 1) if (s ^ lead(b) ^ flip) & 1 == 0 else None)
        )
        yield
        shapes = [struct(((kept.shape[0] - ride) // len(columns), dim), F32)] * len(columns)
        arrays = [near, low]
        if ride:
            shapes.append(struct((8, 128), F32))
        else:
            arrays.append(counts[0])
        yield call(
            functools.partial(rows_kernel, columns, ride), arrays, [], shapes, 6, (), "", "w" * len(columns) + "v"[: ride]
        )

    def block_of(done, bit):
        return part * 2 ** sum(low not in done for low in range(bit))

    def reduce_columns(sent, kept, finish, path):
        got = exchange(sent, path[0])
        yield
        for i in range(1, bits):
            sent, kept = step(kept, got, path[i], block_of(path[:i], path[i]))
            got = exchange(sent, path[i])
            yield
        (low,) = call(both_kernel, [got, kept], [], [struct(kept.shape, BF16)], 4)
        near, far = send_seq(low, 1), send_seq(low, 2)
        yield
        far = hold(far)
        last = send_seq(far, 1)
        yield
        yield finish(last, low, near, far)

    def finish_inner(last, own, near, far):
        return call(
            inner_kernel, [last, counts[0], own, near, far], [place], [struct((part, count * ffn), F32)], 6, (), "", "w"
        )

    def finish_qkv(last, own, near, far):
        return call(
            qkv_kernel,
            [last, counts[0], own, near, far],
            [place],
            [struct((part, dim), F32)] * 3 + [struct((k, part), F32) for k in TAPS] + [struct((part,), F32)] * 2,
            6,
            [pltpu.VMEM((count,) + own.shape, F32)],
            "",
            "w" * 8,
        )

    saved, terms, crossed, lows, grads, sums = [], [], [], [], [], []
    acts, joined, tap_sums, input_terms, inputs = [], [], [], [], []
    outputs = []

    token_parts = [[near, far] for near, far in zip(token_near, token_far)]

    def relay(parts):
        parts[-1] = hold(parts[-1])
        parts.append(send_seq(parts[-1], 1))

    def run_forward(s):
        out, kept = forward(s, token_parts[s])
        terms.append(out)
        saved.append(kept)

    def run_norm(s):
        out, grad, low, norm_sum = normalise(s, *crossed[s], outputs)
        outputs[:] = [out]
        grads.append(grad)
        sums.append(norm_sum)
        lows.append([low, send_seq(low, 1), send_seq(low, 2)])

    def run_backward(s):
        out, acts_s, taps_s = backward(s, joined[s], saved[s])
        input_terms.append(out)
        acts.append(acts_s)
        tap_sums.append(taps_s)

    def run_total(s):
        kept, far = inputs[s]
        totals[:] = call(
            functools.partial(total_kernel, s),
            [far, kept, *totals],
            [],
            [struct((seqs, rows, dim), BF16)],
            4,
            [scratch_of(piece), pltpu.SemaphoreType.DMA],
            "vvh"[: 2 + len(totals)],
            "h",
            [(2, 0)] if totals else [],
        )

    totals = []
    ride = 16 if groups == 2 * count and part % 16 == 0 else 0
    counts = []
    if not ride:
        counted = jnp.pad(jnp.sum(path_masks, axis=0).astype(F32)[None, :], ((0, 7), (0, 128 - path_masks.shape[1])))
        for bit in range(bits):
            counted = counted + exchange(counted, bit)
        counts.append(counted)
    relay(token_parts[0])
    for s in range(seqs):
        run_forward(s)
        if s + 1 < seqs:
            relay(token_parts[s + 1])
        if s > 1:
            relay(lows[s - 2])
            crossed.append(cross(terms[s]))
        if s > 0:
            run_norm(s - 1)
        if s < 2:
            crossed.append(cross(terms[s]))
    for s in range(seqs - 2):
        join(s)
        run_backward(s)
    run_norm(seqs - 1)
    relay(lows[seqs - 2])
    join(seqs - 2)
    inputs = [cross(input_terms[s], grads[s]) for s in range(seqs - 2)]
    mcats = [kept[1] for kept in saved]
    toks = [kept[0] for kept in saved]
    early = slice(0, seqs - 1)
    begun = {
        "o": product(mcats[early], joined[early], (0, ffn), (0, dim)),
        "b": product(mcats[early], joined[early], (ffn, wide), (0, dim)),
    }
    relay(lows[seqs - 1])
    join(seqs - 1)
    path = list(range(bits))
    chunks = {}
    results = {}

    def start(name):
        late = mcats[-1:], joined[-1:]
        if name == "o":
            terms_of = product(*late, (0, ffn), (0, dim), outer_part, 0, (), ride, begun[name])
            chunks[name] = reduce_rows(*terms_of, outer_part, (4,), count // 2, ride)
        elif name == "b":
            terms_of = product(*late, (ffn, wide), (0, dim), part, 0, (), 0, begun[name])
            chunks[name] = reduce_rows(*terms_of, part, (0, 1, 2, 3), 0)
        elif name == "i":
            chunks[name] = reduce_columns(*product(toks, acts, (0, dim), (0, ffn), part), finish_inner, path)
        else:
            terms_of = product(toks, acts, (0, dim), (ffn, act), part, 0, [*tap_sums, *sums])
            chunks[name] = reduce_columns(*terms_of, finish_qkv, path)
        next(chunks[name])

    def advance(name):
        value = next(chunks[name])
        if value is not None:
            results[name] = value
            del chunks[name]
            if name == "o" and ride:
                counts.append(value[-1])

    for name in ORDER:
        if name in "RS":
            run_backward(seqs - 2 + "RS".index(name))
        elif name in "CD":
            s = seqs - 2 + "CD".index(name)
            inputs.append(cross(input_terms[s], grads[s]))
        elif name in "TUV":
            run_total(seqs - 3 + "TUV".index(name))
        elif name.isupper():
            start(name.lower())
        elif name in chunks:
            advance(name)
    while chunks:
        advance(next(iter(chunks)))
    branch_grads = results["b"]
    query_grad, key_grad, value_grad, *kernel_grads, gain_grad, bias_grad = results["q"]
    return (
        outputs[0],
        totals[0],
        query_grad,
        key_grad,
        value_grad,
        branch_grads[0],
        *kernel_grads,
        branch_grads[1],
        branch_grads[2],
        branch_grads[3],
        results["i"][0],
        results["o"][0],
        gain_grad,
        bias_grad,
    )


def solution(mesh):
    rows = P("batch", "seq", None)
    groups = P("batch", None)
    in_specs = (rows, rows, groups, groups) + (P(),) * 14
    out_specs = (
        (rows, rows)
        + (groups,) * 4
        + (P(None, "batch"),) * 3
        + (groups,) * 5
        + (P("batch"), P("batch"))
    )
    body = functools.partial(local, mesh.shape["batch"], mesh.shape["seq"])
    return jax.shard_map(body, mesh=mesh, in_specs=in_specs, out_specs=out_specs, check_vma=False)
```

```python
import functools

import jax
import jax.numpy as jnp
from jax import lax
from jax.experimental import pallas as pl
from jax.experimental.pallas import tpu as pltpu
from jax.sharding import PartitionSpec as P

HD = 64
ORDER = "OBRTCSUDobIQVobiqoibqiobiqobqiq"
PREPARE, FORWARD, BACKWARD, PRODUCT = 6, 8, 10, 8
EPSILON = 1e-05
MASKED = -1e30
TAPS = (3, 5, 7)
F32 = jnp.float32
BF16 = jnp.bfloat16


def dot_nn(left, right):
    return jnp.dot(left, right, preferred_element_type=F32)


def dot_nt(left, right):
    return lax.dot_general(left, right, (((1,), (1,)), ((), ())), preferred_element_type=F32)


def dot_tn(left, right):
    return lax.dot_general(left, right, (((0,), (0,)), ((), ())), preferred_element_type=F32)


def doc_of(starts_ref, row, positions):
    found = jnp.zeros(positions.shape, jnp.int32)
    for which in range(starts_ref.shape[1]):
        found = found + (starts_ref[row, which] <= positions).astype(jnp.int32)
    return found


def assemble(full_ref, pieces, g):
    for k, piece in enumerate(pieces):
        rows = piece.shape[0]
        full_ref[pl.ds(pl.multiple_of((g ^ k) * rows, rows), rows), :] = piece[...]


def spread(part_ref, outs, g):
    for k, out in enumerate(outs):
        rows = out.shape[0]
        out[...] = part_ref[pl.ds(pl.multiple_of((g ^ k) * rows, rows), rows), :].astype(out.dtype)


def documents(doc_ref, starts_ref, which, length, pad):
    position = lax.broadcasted_iota(jnp.int32, (length + 2 * pad, 1), 0) - pad
    found = doc_of(starts_ref, which, position)
    doc_ref[...] = jnp.where(position < length, found, -1)


def channels(out_ref, source, g, count, width, pad):
    length = source.shape[0]
    out_ref[0:pad, :] = jnp.zeros((pad, width), F32)
    out_ref[pad + length : 2 * pad + length, :] = jnp.zeros((pad, width), F32)
    for which in range(count):

        @pl.when(g == which)
        def _():
            out_ref[pad : pad + length, :] = source[:, which * width : (which + 1) * width].astype(F32)


def prepare_kernel(
    count, place_in, query_ref, key_ref, value_ref, inner_ref, outer_ref, output_ref, m3_ref, m5_ref, m7_ref,
    tok_in, cot_in, k3_ref, k5_ref, k7_ref, gain_ref, bias_ref, wcat_ref, wrow_ref, taps_ref, rows_ref, tok_ref, cot_ref, place_ref, buf_ref, sems,
):
    g = place_in[0]
    unit = g ^ (count // 2)
    for i in range(place_ref.shape[0]):
        place_ref[i] = place_in[i]
    dim, ffn = inner_ref.shape[0], inner_ref.shape[1] // count
    width = dim // count
    copies = [
        pltpu.make_async_copy(ref, buf_ref.at[i], sems.at[i]) for i, ref in enumerate((query_ref, key_ref, value_ref))
    ]
    copies.append(
        pltpu.make_async_copy(
            inner_ref.at[:, pl.ds(pl.multiple_of(unit * ffn, ffn), ffn)], wcat_ref.at[:, pl.ds(0, ffn)], sems.at[3]
        )
    )
    copies.append(
        pltpu.make_async_copy(
            outer_ref.at[pl.ds(pl.multiple_of(unit * ffn, ffn), ffn)], wrow_ref.at[pl.ds(0, ffn)], sems.at[4]
        )
    )
    for i, ref in enumerate((output_ref, m3_ref, m5_ref, m7_ref)):
        copies.append(
            pltpu.make_async_copy(
                ref.at[pl.ds(pl.multiple_of(g * width, width), width)],
                wrow_ref.at[pl.ds(ffn + i * width, width)],
                sems.at[5 + i],
            )
        )
    copies.append(pltpu.make_async_copy(tok_in, tok_ref, sems.at[9]))
    copies.append(pltpu.make_async_copy(cot_in, cot_ref, sems.at[10]))
    for copy in copies:
        copy.start()

    rows_ref[...] = jnp.zeros(rows_ref.shape, F32)
    rows_ref[0:1, :] = gain_ref[...].astype(F32).reshape(1, dim)
    rows_ref[1:2, :] = bias_ref[...].astype(F32).reshape(1, dim)
    taps_ref[...] = jnp.zeros(taps_ref.shape, F32)
    for which in range(count):

        @pl.when(g == which)
        def _(which=which):
            at = 0
            for ref in (k3_ref, k5_ref, k7_ref):
                taps = ref[:, which * width : (which + 1) * width].astype(F32)
                taps_ref[at : at + ref.shape[0], :] = taps
                at += ref.shape[0]

    for i in range(3):
        copies[i].wait()
        for which in range(count):

            @pl.when(g == which)
            def _(i=i, which=which):
                wcat_ref[:, ffn + i * width : ffn + (i + 1) * width] = buf_ref[
                    i, :, which * width : (which + 1) * width
                ]

    for copy in copies[3:]:
        copy.wait()


def forward_kernel(
    count, which, g_ref, masks_ref, starts_ref, t0, t1, t2, t3, wcat_ref, wrow_ref, taps_ref,
    p0, p1, p2, p3, tok_ref, mcat_ref, slope_ref, qkv_ref, probs_ref, scaled_ref,
    chan_ref, part_ref, doc_ref,
):
    g = g_ref[0]
    assemble(tok_ref, (t0.at[which], t1, t2, t3), g)
    length, ffn = slope_ref.shape
    width = scaled_ref.shape[1]
    heads = width // HD
    masks = [masks_ref[which, c].astype(F32) for c in range(5)]

    used = [masks_ref[which, c] > 0 for c in range(5)]
    convolved = masks_ref[which, 1] + masks_ref[which, 2] + masks_ref[which, 3] > 0

    @pl.when(used[0])
    def _():
        qkv = dot_nn(tok_ref[...], wcat_ref[:, ffn:]).astype(BF16)
        qkv_ref[:, 0:width] = qkv[:, 0:width] * jnp.asarray(HD**-0.5, BF16)
        qkv_ref[:, width:] = qkv[:, width:]

        linked = doc_of(starts_ref, which, lax.broadcasted_iota(jnp.int32, (length, 1), 0)) == doc_of(
            starts_ref, which, lax.broadcasted_iota(jnp.int32, (1, length), 1)
        )
        ones = jnp.ones((length, HD), BF16)
        for h in range(heads):
            keys = qkv_ref[:, width + h * HD : width + (h + 1) * HD]
            values = jnp.concatenate([qkv_ref[:, 2 * width + h * HD : 2 * width + (h + 1) * HD], ones], axis=1)
            scores = jnp.where(linked, dot_nt(qkv_ref[:, h * HD : (h + 1) * HD], keys), MASKED)
            weights = jnp.exp(scores - jnp.max(scores, axis=1, keepdims=True))
            low = (weights * (1.0 / jnp.sum(weights, axis=1, keepdims=True))).astype(BF16)
            probs_ref[h] = low
            both = dot_nn(low, values)
            attended = both[:, 0:HD]
            scaled_ref[:, h * HD : (h + 1) * HD] = attended / both[:, HD : 2 * HD]
            mcat_ref[:, ffn + h * HD : ffn + (h + 1) * HD] = attended.astype(BF16) * masks[0].astype(BF16)

    @pl.when(jnp.logical_not(used[0]))
    def _():
        mcat_ref[:, ffn : ffn + width] = jnp.zeros((length, width), BF16)
        for ref in (qkv_ref, probs_ref, scaled_ref):
            ref[...] = jnp.zeros(ref.shape, ref.dtype)

    @pl.when(convolved)
    def _():
        pad = 8
        channels(chan_ref, tok_ref, g, count, width, pad)
        documents(doc_ref, starts_ref, which, length, pad)
        tile = min(length, 512)
        for start in range(0, length, tile):
            sums = [jnp.zeros((tile, width), F32) for _ in TAPS]
            docs = doc_ref[pad + start : pad + start + tile, :]
            for shift in range(-3, 4):
                moved = chan_ref[pad + start + shift : pad + start + shift + tile, :]
                if shift != 0:
                    moved = jnp.where(docs == doc_ref[pad + start + shift : pad + start + shift + tile, :], moved, 0.0)
                base = 0
                for k, taps in enumerate(TAPS):
                    if abs(shift) <= taps // 2:
                        tap = base + shift + taps // 2
                        sums[k] = sums[k] + moved * taps_ref[tap : tap + 1, :]
                    base += taps
            for k in range(3):
                lane = ffn + (k + 1) * width
                mcat_ref[start : start + tile, lane : lane + width] = (sums[k] * masks[k + 1]).astype(BF16)

    @pl.when(jnp.logical_not(convolved))
    def _():
        mcat_ref[:, ffn + width :] = jnp.zeros((length, 3 * width), BF16)

    @pl.when(used[4])
    def _():
        tile = min(length, 256)
        for start in range(0, length, tile):
            hidden = dot_nn(tok_ref[start : start + tile, :], wcat_ref[:, 0:ffn])
            cdf = 0.5 + 0.5 * lax.erf(hidden * (0.5**0.5))
            density = jnp.exp(-0.5 * hidden * hidden) * 0.3989422804014327
            mcat_ref[start : start + tile, 0:ffn] = (hidden * cdf * masks[4]).astype(BF16)
            slope_ref[start : start + tile, :] = (cdf + hidden * density).astype(slope_ref.dtype)

    @pl.when(jnp.logical_not(used[4]))
    def _():
        mcat_ref[:, 0:ffn] = jnp.zeros((length, ffn), BF16)
        slope_ref[...] = jnp.zeros(slope_ref.shape, slope_ref.dtype)

    part_ref[...] = dot_nn(mcat_ref[...], wrow_ref[...])
    spread(part_ref, (p0, p1, p2, p3), g)


def norm_kernel(which, *refs):
    kept_ref, far_ref, rows_ref, tok_ref, cot_ref = refs[:5]
    out_all, grad_ref, low_ref, sums_ref, out_ref, sem = refs[-6:]
    summed = tok_ref[which].astype(F32) + (kept_ref[...] + far_ref[...].astype(F32))
    centred = summed - jnp.mean(summed, axis=1, keepdims=True)
    inverse = lax.rsqrt(jnp.mean(centred * centred, axis=1, keepdims=True) + EPSILON)
    normed = centred * inverse
    gain = rows_ref[0:1, :]
    out_ref[...] = (normed * gain + rows_ref[1:2, :]).astype(BF16)
    out_copy = pltpu.make_async_copy(out_ref, out_all.at[which], sem)
    out_copy.start()
    upstream = cot_ref[which].astype(F32)
    sums_ref[...] = jnp.zeros(sums_ref.shape, F32)
    sums_ref[0:1, :] = jnp.sum(upstream * normed, axis=0, keepdims=True)
    sums_ref[1:2, :] = jnp.sum(upstream, axis=0, keepdims=True)
    scaled = upstream * gain
    grad = inverse * (
        scaled
        - jnp.mean(scaled, axis=1, keepdims=True)
        - normed * jnp.mean(scaled * normed, axis=1, keepdims=True)
    )
    grad_ref[...] = grad
    low_ref[...] = grad.astype(BF16)
    out_copy.wait()


def cross_kernel(*refs):
    leaving, away, own, near = refs[:4]
    crossing_ref, kept_ref = refs[-2:]
    crossing_ref[...] = (leaving[...].astype(F32) + away[...].astype(F32)).astype(BF16)
    kept = own[...].astype(F32) + near[...].astype(F32)
    if len(refs) == 7:
        kept = kept + refs[4][...]
    kept_ref[...] = kept


def backward_kernel(
    count, which, g_ref, masks_ref, starts_ref, low_ref, tok_ref, slope_ref, qkv_ref, probs_ref, scaled_ref,
    wcat_ref, wrow_ref, taps_ref,
    p0, p1, p2, p3, acts_ref, tapsum_ref,
    up_ref, chan_ref, c3_ref, c5_ref, c7_ref, part_ref, doc_ref, sums_ref,
):
    g = g_ref[0]
    length, ffn = slope_ref.shape
    width = scaled_ref.shape[1]
    heads = width // HD
    pad = 8
    masks = [masks_ref[which, c].astype(F32) for c in range(5)]

    ups = dot_nt(low_ref[...], wrow_ref[ffn:, :])
    up_ref[...] = (ups[:, 0:width] * masks[0]).astype(BF16)
    conv_refs = (c3_ref, c5_ref, c7_ref)
    for k, ref in enumerate(conv_refs):
        ref[0:pad, :] = jnp.zeros((pad, width), F32)
        ref[pad + length : 2 * pad + length, :] = jnp.zeros((pad, width), F32)
        ref[pad : pad + length, :] = (
            (ups[:, (k + 1) * width : (k + 2) * width] * masks[k + 1]).astype(BF16).astype(F32)
        )

    tile = min(length, 256)
    for start in range(0, length, tile):
        grads = dot_nt(low_ref[start : start + tile, :], wrow_ref[0:ffn, :])
        grads = (grads * masks[4]).astype(BF16).astype(F32)
        acts_ref[start : start + tile, 0:ffn] = (grads * slope_ref[start : start + tile, :].astype(F32)).astype(BF16)

    for h in range(heads):
        keys = qkv_ref[:, width + h * HD : width + (h + 1) * HD]
        values = qkv_ref[:, 2 * width + h * HD : 2 * width + (h + 1) * HD]
        query = qkv_ref[:, h * HD : (h + 1) * HD]
        up = up_ref[:, h * HD : (h + 1) * HD]
        low = probs_ref[h]
        shared = jnp.sum(up.astype(F32) * scaled_ref[:, h * HD : (h + 1) * HD], axis=1, keepdims=True)
        grads = (low.astype(F32) * (dot_nt(up, values) - shared)).astype(BF16)
        lane = ffn + h * HD
        acts_ref[:, lane : lane + HD] = (dot_nn(grads, keys) * (HD**-0.5)).astype(BF16)
        acts_ref[:, lane + width : lane + width + HD] = dot_tn(query, grads).T.astype(BF16)
        acts_ref[:, lane + 2 * width : lane + 2 * width + HD] = dot_tn(up, low).T.astype(BF16)

    part_ref[...] = dot_nt(acts_ref[...], wcat_ref[...])

    tapsum_ref[...] = jnp.zeros(tapsum_ref.shape, F32)

    channels(chan_ref, tok_ref, g, count, width, pad)
    documents(doc_ref, starts_ref, which, length, pad)
    sums_ref[...] = jnp.zeros(sums_ref.shape, F32)
    tile = min(length, 512)
    for start in range(0, length, tile):
        docs = doc_ref[pad + start : pad + start + tile, :]
        own = [ref[pad + start : pad + start + tile, :] for ref in conv_refs]
        back = jnp.zeros((tile, width), F32)
        for shift in range(-3, 4):
            begin = pad + start + shift
            moved = chan_ref[begin : begin + tile, :]
            linked = docs == doc_ref[begin : begin + tile, :]
            if shift != 0:
                moved = jnp.where(linked, moved, 0.0)
            base = 0
            mixed = jnp.zeros((tile, width), F32)
            for k, taps in enumerate(TAPS):
                half = taps // 2
                if abs(shift) <= half:
                    tap = base + shift + half
                    sums_ref[tap] += jnp.sum((own[k] * moved).reshape(tile // 8, 8, width), axis=0)
                    tap = base - shift + half
                    mixed = mixed + conv_refs[k][begin : begin + tile, :] * taps_ref[tap : tap + 1, :]
                base += taps
            back = back + (jnp.where(linked, mixed, 0.0) if shift != 0 else mixed)
        for member in range(count):

            @pl.when(g == member)
            def _(member=member, back=back):
                part_ref[start : start + tile, member * width : (member + 1) * width] += back

    for tap in range(sum(TAPS)):
        tapsum_ref[tap : tap + 1, :] = jnp.sum(sums_ref[tap], axis=0, keepdims=True)
    spread(part_ref, (p0, p1, p2, p3), g)


def join_kernel(place_ref, a, b, c, d, out_ref):
    assemble(out_ref, (a, b, c, d), place_ref[0])


def product_kernel(pairs, take, column, split, bit, spare, ride, begun, g_ref, masks_ref, *refs):
    refs = list(refs)
    lefts, rights, refs = refs[:pairs], refs[pairs : 2 * pairs], refs[2 * pairs :]
    before, refs = (refs[:1], refs[1:]) if begun else ([], refs)
    tapsums, norms, refs = (refs[:pairs], refs[pairs : 2 * pairs], refs[2 * pairs :]) if spare else ([], [], refs)
    if split is None:
        outs, acc_ref = [], refs[0]
    else:
        outs, acc_ref = refs[:2], refs[2]
    g = g_ref[0]
    wide = acc_ref.shape[1] - spare
    for i in range(pairs):
        term = dot_tn(lefts[i][:, take[0] : take[1]], rights[i][:, column[0] : column[1]])
        if i > 0:
            acc_ref[:, 0:wide] += term
        elif begun:
            acc_ref[:, 0:wide] = before[0][...] + term
        else:
            acc_ref[:, 0:wide] = term
    if spare:
        acc_ref[:, wide:] = jnp.zeros((acc_ref.shape[0], spare), F32)
        taps = sum(ref[...] for ref in tapsums).T
        here = pl.ds(pl.multiple_of(g * taps.shape[0], 8), taps.shape[0])
        acc_ref[here, wide : wide + taps.shape[1]] = taps
        norm = sum(ref[...] for ref in norms).T
        acc_ref[:, wide + taps.shape[1] : wide + taps.shape[1] + norm.shape[1]] = norm
    if split is None:
        return
    sent_ref, kept_ref = outs
    mine = (g_ref[1] >> bit) & 1
    if ride:
        lane = lax.broadcasted_iota(jnp.int32, (ride, wide), 1)
        users = jnp.zeros((ride, wide), F32)
        for c in range(masks_ref.shape[1]):
            number = sum(masks_ref[s, c] for s in range(masks_ref.shape[0])).astype(F32)
            users = jnp.where(lane == c, number, users)
        sent_ref[sent_ref.shape[0] - ride :, :] = users.astype(BF16)
        kept_ref[sent_ref.shape[0] - ride :, :] = users
    for j in range((sent_ref.shape[0] - ride) // split):
        start = 2 * j * split
        there = pl.ds(pl.multiple_of(start + (1 - mine) * split, 16), split)
        here = pl.ds(pl.multiple_of(start + mine * split, 16), split)
        sent_ref[j * split : (j + 1) * split, :] = acc_ref[there, :].astype(BF16)
        kept_ref[j * split : (j + 1) * split, :] = acc_ref[here, :]


def step_kernel(block, bit, place_ref, got_ref, kept_ref, sent_ref, rest_ref):
    mine = (place_ref[1] >> bit) & 1
    for j in range(sent_ref.shape[0] // block):
        start = 2 * j * block
        there = pl.ds(pl.multiple_of(start + (1 - mine) * block, 16), block)
        here = pl.ds(pl.multiple_of(start + mine * block, 16), block)
        sent_ref[j * block : (j + 1) * block, :] = (kept_ref[there, :] + got_ref[there, :].astype(F32)).astype(BF16)
        rest_ref[j * block : (j + 1) * block, :] = kept_ref[here, :] + got_ref[here, :].astype(F32)


def add_kernel(got_ref, kept_ref, sum_ref, low_ref):
    total = kept_ref[...] + got_ref[...].astype(F32)
    sum_ref[...] = total
    low_ref[...] = total.astype(BF16)


def own_kernel(which, place_ref, got_ref, kept_ref, low_ref):
    low_ref[...] = jnp.where(place_ref[which] == 1, kept_ref[...] + got_ref[...].astype(F32), 0.0).astype(BF16)


def both_kernel(left_ref, right_ref, out_ref):
    out_ref[...] = (left_ref[...].astype(F32) + right_ref[...].astype(F32)).astype(out_ref.dtype)


def rows_kernel(columns, ride, left_ref, right_ref, *refs):
    outs = refs[len(refs) - len(columns) - (1 if ride else 0) :]
    if ride:
        behind = slice(left_ref.shape[0] - ride, left_ref.shape[0])
        counts = (left_ref[behind, :].astype(F32) + right_ref[behind, :].astype(F32))[0:8, 0:128]
        outs[-1][...] = counts
    else:
        counts = refs[0][...]
    at = 0
    for column, out in zip(columns, outs):
        rows = slice(at, at + out.shape[0])
        total = left_ref[rows, :].astype(F32) + right_ref[rows, :].astype(F32)
        out[...] = total / counts[0:1, column : column + 1]
        at += out.shape[0]


def inner_kernel(g_ref, d, counts_ref, a, b, c, out_ref):
    for k, piece in enumerate((a, b, c, d)):
        lanes = piece.shape[1]
        start = pl.multiple_of((g_ref[0] ^ k ^ 2) * lanes, lanes)
        out_ref[:, pl.ds(start, lanes)] = piece[...].astype(F32) / counts_ref[0:1, 4:5]


def qkv_kernel(g_ref, d, counts_ref, a, b, c, query_ref, key_ref, value_ref, *refs):
    *smalls, gain_out, bias_out, buf_ref = refs
    norm_outs = (gain_out, bias_out)
    pieces = (a, b, c, d)
    for k, piece in enumerate(pieces):
        buf_ref[g_ref[0] ^ k] = piece[...].astype(F32)
    width = query_ref.shape[1] // len(pieces)
    for i, out in enumerate((query_ref, key_ref, value_ref)):
        for m in range(len(pieces)):
            out[:, m * width : (m + 1) * width] = buf_ref[m, :, i * width : (i + 1) * width] / counts_ref[0:1, 0:1]
    spare = sum(buf_ref[m, :, 3 * width :] for m in range(len(pieces))).T
    at = 0
    for i, out in enumerate(smalls):
        out[...] = spare[at : at + out.shape[0], :] / counts_ref[0:1, i + 1 : i + 2]
        at += out.shape[0]
    for i, out in enumerate(norm_outs):
        out[...] = spare[at + 1 + i : at + 2 + i, :].reshape(out.shape)


def total_kernel(which, *refs):
    far_ref, kept_ref = refs[:2]
    out_all, out_ref, sem = refs[-3:]
    out_ref[...] = (kept_ref[...] + far_ref[...].astype(F32)).astype(BF16)
    copy = pltpu.make_async_copy(out_ref, out_all.at[which], sem)
    copy.start()
    copy.wait()


def smem():
    return pl.BlockSpec(memory_space=pltpu.SMEM)


def struct(shape, dtype):
    return jax.ShapeDtypeStruct(tuple(shape), dtype)


def scratch_of(shape):
    return pltpu.VMEM(shape.shape, shape.dtype)


def local(
    groups, count, tokens, cotangent, path_masks, seg_starts, query_weight, key_weight, value_weight, output_weight,
    small_kernel, middle_kernel, large_kernel, small_mixer, middle_mixer, large_mixer, inner_weight, outer_weight,
    norm_gain, norm_bias,
):
    seqs, rows, dim = tokens.shape
    length = rows * count
    width = dim // count
    ffn = inner_weight.shape[1] // count
    wide = ffn + 4 * width
    act = ffn + 3 * width
    heads = width // HD
    part = dim // groups
    outer_part = part * ffn // width
    bits = groups.bit_length() - 1
    top = count.bit_length() - 1
    batch, g = lax.axis_index("batch").astype(jnp.int32), lax.axis_index("seq").astype(jnp.int32)
    owner = batch >> (bits - top)
    place = jnp.stack([g, batch, (owner == g).astype(jnp.int32), (owner == g ^ (count // 2)).astype(jnp.int32)])

    turn = []

    def call(kernel, arrays, scalars, out_shape, limit, scratch=(), ins="", outs="", aliases=()):
        ins = ins + "v" * (len(arrays) - len(ins))
        outs = outs + "v" * (len(out_shape) - len(outs))
        before = len(scalars) + len(arrays)
        behind = list(turn)

        def body(*refs):
            kernel(*refs[:before], *refs[before + len(behind) :])

        def seen(kinds):
            spaces = {"h": pltpu.HBM, "s": pltpu.SMEM}
            return [pl.BlockSpec(memory_space=spaces.get(kind, pltpu.VMEM)) for kind in kinds]

        def home(kind):
            return pltpu.VMEM if kind == "v" else pltpu.HBM

        def lies(x, kind):
            return pltpu.with_memory_space_constraint(x, home(kind))

        out = pl.pallas_call(
            body,
            in_specs=[smem()] * len(scalars) + seen(ins) + [pl.BlockSpec(memory_space=pl.ANY)] * len(behind),
            out_specs=seen(outs),
            out_shape=[home(kind)(x.shape, x.dtype) for kind, x in zip(outs, out_shape)],
            scratch_shapes=list(scratch),
            input_output_aliases={len(scalars) + i: o for i, o in aliases},
            compiler_params=pltpu.CompilerParams(vmem_limit_bytes=limit * 1024 * 1024),
            cost_estimate=pl.CostEstimate(flops=1000, bytes_accessed=1000, transcendentals=0),
        )(
            *[lies(x, "h") for x in scalars],
            *[lies(x, kind) for x, kind in zip(arrays, ins)],
            *[lies(x, kind) for x, kind in behind],
        )
        smallest = min((i for i in range(len(out)) if outs[i] != "s"), key=lambda i: out[i].size)
        turn[:] = [(out[smallest], outs[smallest])]
        return out

    def hold(value):
        return call(lambda *refs: None, [value], [], [struct(value.shape, value.dtype)], 1, aliases=[(0, 0)])[0]

    turned = []

    def listed(found):
        turned.append(None)
        at = len(turned) % len(found)
        return found[at:] + found[:at]

    def send_seq(value, flip):
        return lax.ppermute(value, "seq", listed([(i, i ^ flip) for i in range(count)]))

    def exchange(sent, bit):
        return lax.ppermute(sent, "batch", listed([(i, i ^ (1 << bit)) for i in range(groups)]))

    def lead(b):
        return b >> (bits - top)

    def pairs(want):
        found = []
        for b in range(groups):
            for s in range(count):
                to = want(b, s)
                if to is not None:
                    found.append((b * count + s, to[0] * count + to[1]))
        return listed(found)

    piece = struct((rows, dim), BF16)
    full = struct((length, dim), BF16)
    pads = pltpu.VMEM((length + 16, width), F32)

    token_near = [send_seq(tokens[s], 1) for s in range(seqs)]
    token_far = [send_seq(tokens[s], 2) for s in range(seqs)]
    tap_rows = sum(TAPS) + 1
    wcat, wrow, taps, norm_rows, tokens_here, cotangent_here, place = call(
        functools.partial(prepare_kernel, count),
        [
            query_weight, key_weight, value_weight, inner_weight, outer_weight, output_weight, small_mixer,
            middle_mixer, large_mixer, tokens, cotangent, small_kernel, middle_kernel, large_kernel, norm_gain, norm_bias,
        ],
        [place],
        [
            struct((dim, act), BF16), struct((wide, dim), BF16), struct((tap_rows, width), F32), struct((8, dim), F32),
            struct(tokens.shape, BF16), struct(tokens.shape, BF16), struct(place.shape, jnp.int32),
        ],
        PREPARE,
        [pltpu.VMEM((3, dim, dim), BF16), pltpu.SemaphoreType.DMA((11,))],
        "h" * 11 + "w" * 5,
        "vvvvvvs",
    )

    saved_shapes = [
        full,
        struct((length, wide), BF16),
        struct((length, ffn), BF16),
        struct((length, 3 * width), BF16),
        struct((heads, length, length), BF16),
        struct((length, width), F32),
    ]

    def forward(s, parts):
        p0, p1, p2, p3, *kept = call(
            functools.partial(forward_kernel, count, s),
            [tokens_here, *parts, wcat, wrow, taps],
            [place, path_masks, seg_starts],
            [piece] * 4 + saved_shapes,
            FORWARD,
            [pads, pltpu.VMEM((length, dim), F32), pltpu.VMEM((length + 16, 1), jnp.int32)],
        )
        return (p2, send_seq(p3, 1), p0, send_seq(p1, 1)), kept

    def cross(terms, grad=None):
        more = [] if grad is None else [grad]
        crossing, kept = call(
            cross_kernel, [*terms, *more], [], [piece, struct((rows, dim), F32)], 4
        )
        return kept, send_seq(crossing, 2)

    def normalise(s, kept, far, outputs):
        return call(
            functools.partial(norm_kernel, s),
            [kept, far, norm_rows, tokens_here, cotangent_here, *outputs],
            [],
            [struct((seqs, rows, dim), BF16), struct((rows, dim), F32), piece, struct((8, dim), F32)],
            4,
            [scratch_of(piece), pltpu.SemaphoreType.DMA],
            "vvvvvh"[: 5 + len(outputs)],
            "hvvv",
            [(5, 0)] if outputs else [],
        )

    def join(s):
        (whole,) = call(join_kernel, lows[s], [place], [full], 4)
        joined.append(whole)

    def backward(s, low_full, kept):
        tok_full, _, slope, qkv, probs, scaled = kept
        p0, p1, p2, p3, acts, taps_sum = call(
            functools.partial(backward_kernel, count, s),
            [low_full, tok_full, slope, qkv, probs, scaled, wcat, wrow, taps],
            [place, path_masks, seg_starts],
            [piece] * 4 + [struct((length, act), BF16), struct(taps.shape, F32)],
            BACKWARD,
            [pltpu.VMEM((length, width), BF16)]
            + [pads] * 4
            + [
                pltpu.VMEM((length, dim), F32), pltpu.VMEM((length + 16, 1), jnp.int32),
                pltpu.VMEM((tap_rows, 8, width), F32),
            ],
        )
        return (p2, send_seq(p3, 1), p0, send_seq(p1, 1)), acts, taps_sum

    def product(lefts, rights, take, column, block=None, bit=0, beside=(), ride=0, begun=()):
        m, w = take[1] - take[0], column[1] - column[0]
        spare = -w % 128 if beside else 0
        split = block if block and block % 16 == 0 else None
        acc = struct((m, w + spare), F32)
        shapes = [acc] if split is None else [struct((m // 2 + ride, w + spare), BF16), struct((m // 2 + ride, w + spare), F32)]
        out = call(
            functools.partial(product_kernel, len(lefts), take, column, split, bit, spare, ride, len(begun)),
            [*lefts, *rights, *begun, *beside],
            [place, path_masks],
            shapes,
            PRODUCT,
            [] if split is None else [scratch_of(acc)],
        )
        if split is not None or not block:
            return out
        return halves(out[0], bit, block)

    def halves(value, bit, block):
        m, w = value.shape
        split = value.reshape(m // (2 * block), 2, block, w)
        mine = (batch >> bit) & 1
        sent = lax.dynamic_index_in_dim(split, 1 - mine, axis=1, keepdims=False)
        kept = lax.dynamic_index_in_dim(split, mine, axis=1, keepdims=False)
        return sent.reshape(m // 2, w).astype(BF16), kept.reshape(m // 2, w)

    def step(kept, got, bit, block):
        m, w = kept.shape
        if block % 16 != 0:
            return halves(kept + got.astype(F32), bit, block)
        return call(
            functools.partial(step_kernel, block, bit),
            [got, kept],
            [place],
            [struct((m // 2, w), BF16), struct((m // 2, w), F32)],
            4,
        )

    def reduce_rows(sent, kept, block, columns, flip, ride=0):
        got = exchange(sent, 0)
        yield
        for bit in range(1, bits - top):
            sent, kept = step(kept, got, bit, block)
            got = exchange(sent, bit)
            yield
        for bit in range(top):
            level = bits - top + bit

            def target(b, s, bit=bit, level=level):
                settled = (lead(b) ^ s ^ flip) & ((1 << bit) - 1)
                if settled or not ((lead(b) ^ s ^ flip) >> bit) & 1:
                    return None
                return b ^ (1 << level), s

            kept, sent = call(add_kernel, [got, kept], [], [struct(kept.shape, F32), struct(kept.shape, BF16)], 4)
            got = lax.ppermute(sent, ("batch", "seq"), pairs(target))
            yield
        (low,) = call(functools.partial(own_kernel, 3 if flip else 2), [got, kept], [place], [struct(kept.shape, BF16)], 4)
        far = lax.ppermute(low, ("batch", "seq"), pairs(lambda b, s: (b, s ^ 2) if s == lead(b) ^ flip else None))
        yield
        (low,) = call(both_kernel, [far, low], [], [struct(kept.shape, BF16)], 4)
        near = lax.ppermute(
            low, ("batch", "seq"), pairs(lambda b, s: (b, s ^ 1) if (s ^ lead(b) ^ flip) & 1 == 0 else None)
        )
        yield
        shapes = [struct(((kept.shape[0] - ride) // len(columns), dim), F32)] * len(columns)
        arrays = [near, low]
        if ride:
            shapes.append(struct((8, 128), F32))
        else:
            arrays.append(counts[0])
        yield call(
            functools.partial(rows_kernel, columns, ride), arrays, [], shapes, 6, (), "", "w" * len(columns) + "v"[: ride]
        )

    def block_of(done, bit):
        return part * 2 ** sum(low not in done for low in range(bit))

    def reduce_columns(sent, kept, finish, path):
        got = exchange(sent, path[0])
        yield
        for i in range(1, bits):
            sent, kept = step(kept, got, path[i], block_of(path[:i], path[i]))
            got = exchange(sent, path[i])
            yield
        (low,) = call(both_kernel, [got, kept], [], [struct(kept.shape, BF16)], 4)
        near, far = send_seq(low, 1), send_seq(low, 2)
        yield
        far = hold(far)
        last = send_seq(far, 1)
        yield
        yield finish(last, low, near, far)

    def finish_inner(last, own, near, far):
        return call(
            inner_kernel, [last, counts[0], own, near, far], [place], [struct((part, count * ffn), F32)], 6, (), "", "w"
        )

    def finish_qkv(last, own, near, far):
        return call(
            qkv_kernel,
            [last, counts[0], own, near, far],
            [place],
            [struct((part, dim), F32)] * 3 + [struct((k, part), F32) for k in TAPS] + [struct((part,), F32)] * 2,
            6,
            [pltpu.VMEM((count,) + own.shape, F32)],
            "",
            "w" * 8,
        )

    saved, terms, crossed, lows, grads, sums = [], [], [], [], [], []
    acts, joined, tap_sums, input_terms, inputs = [], [], [], [], []
    outputs = []

    token_parts = [[near, far] for near, far in zip(token_near, token_far)]

    def relay(parts):
        parts[-1] = hold(parts[-1])
        parts.append(send_seq(parts[-1], 1))

    def run_forward(s):
        out, kept = forward(s, token_parts[s])
        terms.append(out)
        saved.append(kept)

    def run_norm(s):
        out, grad, low, norm_sum = normalise(s, *crossed[s], outputs)
        outputs[:] = [out]
        grads.append(grad)
        sums.append(norm_sum)
        lows.append([low, send_seq(low, 1), send_seq(low, 2)])

    def run_backward(s):
        out, acts_s, taps_s = backward(s, joined[s], saved[s])
        input_terms.append(out)
        acts.append(acts_s)
        tap_sums.append(taps_s)

    def run_total(s):
        kept, far = inputs[s]
        totals[:] = call(
            functools.partial(total_kernel, s),
            [far, kept, *totals],
            [],
            [struct((seqs, rows, dim), BF16)],
            4,
            [scratch_of(piece), pltpu.SemaphoreType.DMA],
            "vvh"[: 2 + len(totals)],
            "h",
            [(2, 0)] if totals else [],
        )

    totals = []
    ride = 16 if groups == 2 * count and part % 16 == 0 else 0
    counts = []
    if not ride:
        counted = jnp.pad(jnp.sum(path_masks, axis=0).astype(F32)[None, :], ((0, 7), (0, 128 - path_masks.shape[1])))
        for bit in range(bits):
            counted = counted + exchange(counted, bit)
        counts.append(counted)
    relay(token_parts[0])
    for s in range(seqs):
        run_forward(s)
        if s + 1 < seqs:
            relay(token_parts[s + 1])
        if s > 1:
            relay(lows[s - 2])
        if s > 0:
            run_norm(s - 1)
        crossed.append(cross(terms[s]))
    for s in range(seqs - 2):
        join(s)
        run_backward(s)
    run_norm(seqs - 1)
    relay(lows[seqs - 2])
    join(seqs - 2)
    inputs = [cross(input_terms[s], grads[s]) for s in range(seqs - 2)]
    mcats = [kept[1] for kept in saved]
    toks = [kept[0] for kept in saved]
    early = slice(0, seqs - 1)
    begun = {
        "o": product(mcats[early], joined[early], (0, ffn), (0, dim)),
        "b": product(mcats[early], joined[early], (ffn, wide), (0, dim)),
    }
    relay(lows[seqs - 1])
    join(seqs - 1)
    path = list(range(bits))
    chunks = {}
    results = {}

    def start(name):
        late = mcats[-1:], joined[-1:]
        if name == "o":
            terms_of = product(*late, (0, ffn), (0, dim), outer_part, 0, (), ride, begun[name])
            chunks[name] = reduce_rows(*terms_of, outer_part, (4,), count // 2, ride)
        elif name == "b":
            terms_of = product(*late, (ffn, wide), (0, dim), part, 0, (), 0, begun[name])
            chunks[name] = reduce_rows(*terms_of, part, (0, 1, 2, 3), 0)
        elif name == "i":
            chunks[name] = reduce_columns(*product(toks, acts, (0, dim), (0, ffn), part), finish_inner, path)
        else:
            terms_of = product(toks, acts, (0, dim), (ffn, act), part, 0, [*tap_sums, *sums])
            chunks[name] = reduce_columns(*terms_of, finish_qkv, path)
        next(chunks[name])

    def advance(name):
        value = next(chunks[name])
        if value is not None:
            results[name] = value
            del chunks[name]
            if name == "o" and ride:
                counts.append(value[-1])

    for name in ORDER:
        if name in "RS":
            run_backward(seqs - 2 + "RS".index(name))
        elif name in "CD":
            s = seqs - 2 + "CD".index(name)
            inputs.append(cross(input_terms[s], grads[s]))
        elif name in "TUV":
            run_total(seqs - 3 + "TUV".index(name))
        elif name.isupper():
            start(name.lower())
        elif name in chunks:
            advance(name)
    while chunks:
        advance(next(iter(chunks)))
    branch_grads = results["b"]
    query_grad, key_grad, value_grad, *kernel_grads, gain_grad, bias_grad = results["q"]
    return (
        outputs[0],
        totals[0],
        query_grad,
        key_grad,
        value_grad,
        branch_grads[0],
        *kernel_grads,
        branch_grads[1],
        branch_grads[2],
        branch_grads[3],
        results["i"][0],
        results["o"][0],
        gain_grad,
        bias_grad,
    )


def solution(mesh):
    rows = P("batch", "seq", None)
    groups = P("batch", None)
    in_specs = (rows, rows, groups, groups) + (P(),) * 14
    out_specs = (
        (rows, rows)
        + (groups,) * 4
        + (P(None, "batch"),) * 3
        + (groups,) * 5
        + (P("batch"), P("batch"))
    )
    body = functools.partial(local, mesh.shape["batch"], mesh.shape["seq"])
    return jax.shard_map(body, mesh=mesh, in_specs=in_specs, out_specs=out_specs, check_vma=False)
```
